512 devices in a mesh: gx: 8 (over z_lo, x), gy: 4 (over z_hi), gz: 16 (over y, core).
Axes of the slice: x: 4, y: 8, z: 8 (z_hi: 4, z_lo: 2; z = z_hi * 2 + z_lo), core: 2. Of those that a mesh axis runs over, the one named last changes fastest.
Arguments:
- body_load: float32 [3, 32, 64, 2048], P(None, 'gx', 'gy', 'gz'), may hold values from -24 to 24
- contact_mask: int32 [32, 64, 2048], P('gx', 'gy', 'gz'), may hold values 0 or 1
- contact_gap: float32 [32, 64, 2048], P('gx', 'gy', 'gz'), may hold values from 0.1 to 0.8
- material_ids: int32 [32, 64, 2048], P('gx', 'gy', 'gz'), may hold values from 0 to 3
- lame_table: float32 [4, 2], replicated, may hold values from 0.5 to 2
Outputs:
- displacement: float32 [3, 32, 64, 2048], P(None, 'gx', 'gy', 'gz')
- multiplier: float32 [3, 32, 64, 2048], P(None, 'gx', 'gy', 'gz')
- gap_history: float32 [6], replicated
The draws below stay inside these ranges and needn't reach their ends.
All inputs are finite; a program needn't handle non-finite values. No bound on the sum of `contact_mask` on one device may be relied on, other than what follows from the above.
Results may differ from the reference program's by a relative error of at most 0.0001.
Values sent between devices are 32-bit elements; how exact they have to be, the bound alone decides.
No kernel may reach another device: no remote copies, remote signals or barrier semaphores. Data moves between devices by JAX's collectives and lax.ppermute only.
A program may use at most 64 MiB of HBM per device.

```python
import math
import jax
import jax.numpy as jnp
import numpy as np
from jax import lax

CX = 4
ITERS = 6
NMAT = 4
NX = 32
NY = 64
NZ = 2048


def place_ends(values, stream_key, low, high):
    place = [jax.random.randint(jax.random.fold_in(stream_key, axis), (), 0, length) for axis, length in enumerate(values.shape)]
    longest = values.shape.index(max(values.shape))
    neighbour = place[:longest] + [(place[longest] + 1) % values.shape[longest]] + place[longest + 1:]
    return values.at[tuple(place)].set(low).at[tuple(neighbour)].set(high)


def shard_levels(key, dims, cuts, least, top_value):
    level, own = 1.0, jax.random.fold_in(key, 6)
    for dim, shards_of in cuts:
        draws = jnp.exp(jax.random.uniform(jax.random.fold_in(own, dim), (shards_of,), jnp.float32, least / len(cuts), top_value / len(cuts)))
        level = level * jnp.repeat(draws, dims[dim] // shards_of).reshape([-1 if axis == dim else 1 for axis in range(len(dims))])
    return level


def noise(stream_key, dims, scale, limit, cuts=(), kind=jnp.bfloat16):
    values = jax.random.normal(stream_key, dims, jnp.float32) * scale
    if len(cuts) > 0:
        values = shard_levels(stream_key, dims, cuts, -0.22, 0.18) * values
    return jnp.clip(values, min=-limit, max=limit).astype(kind)


def setup_inputs(seed: int = 0) -> dict:
    arg_keys = jax.random.split(jax.random.key(seed), 6)
    return {
        "body_load": noise(arg_keys[0], (3, NX, NY, NZ), 4.0, 24.0, ((1, 8), (2, 4), (3, 16)), jnp.float32),
        "contact_mask": place_ends((jax.random.randint(arg_keys[1], (NX, NY, NZ), 0, 3) < 1).astype(jnp.int32), jax.random.fold_in(arg_keys[1], 1), 0, 1),
        "contact_gap": jnp.clip(0.1 + 0.7 * jax.random.uniform(arg_keys[2], (NX, NY, NZ), jnp.float32) ** shard_levels(arg_keys[2], (NX, NY, NZ), ((0, 8), (1, 4), (2, 16)), -0.2, 0.2), 0.1, 0.8),
        "material_ids": place_ends(jax.random.randint(arg_keys[3], (NX, NY, NZ), 0, NMAT), jax.random.fold_in(arg_keys[3], 1), 0, NMAT - 1).astype(jnp.int32),
        "lame_table": jnp.clip(jnp.exp(jax.random.uniform(arg_keys[4], (NMAT, 2), jnp.float32, math.log(0.5), math.log(2.0))), 0.5, 2.0),
    }


def corner_offsets(a):
    return ((a >> 2) & 1, (a >> 1) & 1, a & 1)


def element_tables():
    points = np.array([(1.0 - 3.0 ** -0.5) / 2.0, (1.0 + 3.0 ** -0.5) / 2.0])
    stiff_lame = np.zeros((24, 24))
    stiff_shear = np.zeros((24, 24))
    for p in points:
        for q in points:
            for r in points:
                position = (p, q, r)
                gradients = np.zeros((8, 3))
                for a in range(8):
                    corner = corner_offsets(a)
                    for d in range(3):
                        factor = 1.0
                        for e in range(3):
                            if e == d:
                                factor = factor * (1.0 if corner[e] else -1.0)
                            else:
                                factor = factor * (position[e] if corner[e] else 1.0 - position[e])
                        gradients[a, d] = factor
                for a in range(8):
                    for c in range(3):
                        for b in range(8):
                            for d in range(3):
                                stiff_lame[3 * a + c, 3 * b + d] += 0.125 * gradients[a, c] * gradients[b, d]
                                stiff_shear[3 * a + c, 3 * b + d] += 0.125 * (float(c == d) * np.dot(gradients[a], gradients[b]) + gradients[a, d] * gradients[b, c])
    return stiff_lame, stiff_shear


def material_fields(material_ids, lame_table):
    first = jnp.zeros(material_ids.shape, jnp.float32)
    shear = jnp.zeros(material_ids.shape, jnp.float32)
    for m in range(lame_table.shape[0]):
        hit = material_ids == m
        first = jnp.where(hit, lame_table[m, 0], first)
        shear = jnp.where(hit, lame_table[m, 1], shear)
    return first, shear


def element_forces(nodes, first, shear, kboth, counts):
    ecx, ecy, ecz = counts
    corners = []
    for a in range(8):
        o = corner_offsets(a)
        corners.append(nodes[:, o[0]:o[0] + ecx, o[1]:o[1] + ecy, o[2]:o[2] + ecz])
    stacked = jnp.stack(corners, 0).reshape(24, ecx * ecy * ecz)
    product = jnp.dot(kboth, stacked, precision=lax.Precision.HIGHEST, preferred_element_type=jnp.float32)
    result = first[:ecx, :ecy, :ecz].reshape(-1) * product[:24] + shear[:ecx, :ecy, :ecz].reshape(-1) * product[24:]
    return result.reshape(8, 3, ecx, ecy, ecz)


def assemble(forces, counts):
    ncx, ncy, ncz = counts
    total = None
    for a in range(8):
        o = corner_offsets(a)
        piece = forces[a][:, 1 - o[0]:1 - o[0] + ncx, 1 - o[1]:1 - o[1] + ncy, 1 - o[2]:1 - o[2] + ncz]
        total = piece if total is None else total + piece
    return total


def reference(body_load, contact_mask, contact_gap, material_ids, lame_table):
    stiff_lame, stiff_shear = element_tables()
    kboth = jnp.asarray(np.concatenate([stiff_lame, stiff_shear], 0), jnp.float32)
    lame_rows = float(np.max(np.sum(np.abs(stiff_lame), 1)))
    shear_rows = float(np.max(np.sum(np.abs(stiff_shear), 1)))
    bound = 8.0 * jnp.max(lame_table[:, 0] * lame_rows + lame_table[:, 1] * shear_rows)
    step_size = 1.5 / (1.0 + bound)
    first, shear = material_fields(material_ids, lame_table)
    first_ext = jnp.pad(first, ((1, 0), (1, 0), (1, 0)), mode="wrap")
    shear_ext = jnp.pad(shear, ((1, 0), (1, 0), (1, 0)), mode="wrap")
    slab = CX
    starts = jnp.arange(NX // slab, dtype=jnp.int32) * slab

    def apply_stiffness(displace):
        padded = jnp.pad(displace, ((0, 0), (1, 1), (1, 1), (1, 1)), mode="wrap")

        def one_slab(start):
            zero = jnp.zeros((), jnp.int32)
            nodes = lax.dynamic_slice(padded, (zero, start, zero, zero), (3, slab + 2, NY + 2, NZ + 2))
            first_slab = lax.dynamic_slice(first_ext, (start, zero, zero), (slab + 1, NY + 1, NZ + 1))
            shear_slab = lax.dynamic_slice(shear_ext, (start, zero, zero), (slab + 1, NY + 1, NZ + 1))
            forces = element_forces(nodes, first_slab, shear_slab, kboth, (slab + 1, NY + 1, NZ + 1))
            return assemble(forces, (slab, NY, NZ))

        stacked = lax.map(one_slab, starts)
        return jnp.moveaxis(stacked, 0, 1).reshape(3, NX, NY, NZ)

    primal = jnp.zeros(body_load.shape, jnp.float32)
    split = jnp.zeros(body_load.shape, jnp.float32)
    scaled_dual = jnp.zeros(body_load.shape, jnp.float32)
    history = []
    for t in range(ITERS):
        forces = apply_stiffness(primal)
        primal = primal - step_size * (forces - body_load + (primal - split + scaled_dual))
        shifted = primal + scaled_dual
        bounded = jnp.where(contact_mask > 0, jnp.maximum(shifted[2], -contact_gap), shifted[2])
        split = jnp.concatenate([shifted[:2], bounded[None]], 0)
        scaled_dual = shifted - split
        history.append(jnp.max(jnp.abs(primal - split)))
    return primal, scaled_dual, jnp.stack(history)
```

```python
import jax
import jax.numpy as jnp
import numpy as np
from jax import lax
from jax.experimental import pallas as pl
from jax.experimental.pallas import tpu as pltpu
from jax.sharding import PartitionSpec as P

ITERS = 6
DEPTH = ITERS - 1
SWAP = ("gy", "gx")
CHUNK = 4
WIDE = CHUNK + 2 * DEPTH
SLOT = 40
BACK = 16
LOWEST = float(np.finfo(np.float32).min)


def corner_offsets(a):
    return (a >> 2 & 1, a >> 1 & 1, a & 1)


def element_tables():
    points = np.array([(1.0 - 3.0 ** (-0.5)) / 2.0, (1.0 + 3.0 ** (-0.5)) / 2.0])
    stiff_lame = np.zeros((24, 24))
    stiff_shear = np.zeros((24, 24))
    for p in points:
        for q in points:
            for r in points:
                position = (p, q, r)
                gradients = np.zeros((8, 3))
                for a in range(8):
                    corner = corner_offsets(a)
                    for d in range(3):
                        factor = 1.0
                        for e in range(3):
                            if e == d:
                                factor = factor * (1.0 if corner[e] else -1.0)
                            else:
                                factor = factor * (position[e] if corner[e] else 1.0 - position[e])
                        gradients[a, d] = factor
                for a in range(8):
                    for c in range(3):
                        for b in range(8):
                            for d in range(3):
                                stiff_lame[3 * a + c, 3 * b + d] += (
                                    0.125 * gradients[a, c] * gradients[b, d]
                                )
                                stiff_shear[3 * a + c, 3 * b + d] += 0.125 * (
                                    float(c == d) * np.dot(gradients[a], gradients[b])
                                    + gradients[a, d] * gradients[b, c]
                                )
    return (stiff_lame, stiff_shear)


def bounds():
    stiff_lame, stiff_shear = element_tables()
    return (
        float(np.max(np.sum(np.abs(stiff_lame), 1))),
        float(np.max(np.sum(np.abs(stiff_shear), 1))),
    )


def turn_kernel(load_ref, mask_ref, gap_ref, ids_ref, rows_ref, first_ref, last_ref):
    flat = lambda v: v.reshape(64, 128)
    low = jnp.where(mask_ref[...] > 0, -gap_ref[...], LOWEST)
    low = flat(low)
    ids = flat(ids_ref[...].astype(jnp.float32))
    pairs = (
        (flat(load_ref[0]), flat(load_ref[1])),
        (flat(load_ref[2]), ids),
        (low, low),
    )
    for i, pair in enumerate(pairs):
        turned = jnp.concatenate(pair, 0).T
        rows_ref[i] = turned
        first_ref[i] = turned[:8]
        last_ref[i] = turned[120:]


def slots_kernel(rows_ref, before_ref, after_ref, out_ref, wide):
    for i in range(3):
        wide[i, 0:8] = before_ref[i]
        wide[i, 8:136] = rows_ref[i]
        wide[i, 136:144] = after_ref[i]
    lower = lax.broadcasted_iota(jnp.int32, (6, 128), 1) < 64
    for d in range(32):
        at = CHUNK * d + 8 - DEPTH
        out_ref[d, 0:WIDE] = wide[0, at : at + WIDE]
        out_ref[d, 16 : 16 + WIDE] = wide[1, at : at + WIDE]
        out_ref[d, 32:38] = jnp.where(
            lower, wide[2, at + 1 : at + 7], wide[2, at + 7 : at + 13]
        )


def flip(v, even):
    return jnp.where(even, pltpu.roll(v, 7, 0), pltpu.roll(v, 1, 0))


def make_shifts():
    lane = lax.broadcasted_iota(jnp.int32, (8, 128), 1)
    even = lax.broadcasted_iota(jnp.int32, (8, 128), 0) % 2 == 0
    top_x, low_x = lane >= 112, lane < 16
    top_y, low_y = lane % 16 == 15, lane % 16 == 0

    def x_up(v):
        r0, r1 = pltpu.roll(v[0], 112, 1), pltpu.roll(v[1], 112, 1)
        return (jnp.where(top_x, r1, r0), jnp.where(top_x, flip(r0, even), r1))

    def x_down(v):
        r0, r1 = pltpu.roll(v[0], 16, 1), pltpu.roll(v[1], 16, 1)
        return (jnp.where(low_x, flip(r1, even), r0), jnp.where(low_x, r0, r1))

    def y_up(v):
        return tuple(
            jnp.where(top_y, pltpu.roll(pltpu.roll(a, 6, 0), 15, 1), pltpu.roll(a, 127, 1))
            for a in v
        )

    def y_down(v):
        return tuple(
            jnp.where(low_y, pltpu.roll(pltpu.roll(a, 2, 0), 113, 1), pltpu.roll(a, 1, 1))
            for a in v
        )

    return (x_up, x_down, y_up, y_down)


def add(a, b):
    return tuple(i + j for i, j in zip(a, b))


def sub(a, b):
    return tuple(i - j for i, j in zip(a, b))


def element(low, high, lam, mu):
    s = [[h + l for l, h in zip(low[c], high[c])] for c in range(3)]
    d = [[h - l for l, h in zip(low[c], high[c])] for c in range(3)]
    lam3, mu3, mu2 = lam * (1.0 / 3.0), mu * (1.0 / 3.0), mu + mu
    last = (lam + 4.0 * mu) * (1.0 / 9.0)
    SS, DS, SD, DD = range(4)
    fs = [[None] * 4 for _ in range(3)]
    fd = [[None] * 4 for _ in range(3)]
    exx, eyy, ezz = s[0][DS], s[1][SD], d[2][SS]
    trace = lam * (exx + eyy + ezz)
    fs[0][DS] = trace + mu2 * exx
    fs[1][SD] = trace + mu2 * eyy
    fd[2][SS] = trace + mu2 * ezz
    fs[0][SD] = fs[1][DS] = mu * (s[0][SD] + s[1][DS])
    fd[0][SS] = fs[2][DS] = mu * (d[0][SS] + s[2][DS])
    fd[1][SS] = fs[2][SD] = mu * (d[1][SS] + s[2][SD])
    both = lam3 * (s[0][DD] + d[2][SD])
    fs[0][DD] = both + mu * s[0][DD]
    fd[2][SD] = both + mu * d[2][SD]
    both = lam3 * (s[1][DD] + d[2][DS])
    fs[1][DD] = both + mu * s[1][DD]
    fd[2][DS] = both + mu * d[2][DS]
    both = lam3 * (d[0][DS] + d[1][SD])
    fd[0][DS] = both + mu * d[0][DS]
    fd[1][SD] = both + mu * d[1][SD]
    total = s[2][DD] + d[1][DS] + d[0][SD]
    fs[2][DD] = mu3 * (total + s[2][DD])
    fd[1][DS] = mu3 * (total + d[1][DS])
    fd[0][SD] = mu3 * (total + d[0][SD])
    for c in range(3):
        fd[c][DD] = last * d[c][DD]
    down = [[-fd[c][0]] + [fs[c][m] - fd[c][m] for m in (1, 2, 3)] for c in range(3)]
    up = [[fd[c][0]] + [fs[c][m] + fd[c][m] for m in (1, 2, 3)] for c in range(3)]
    return (down, up)


def iterate_kernel(gl, gm, table_ref, in_ref, out_ref, u, u1, quad, dual, low, lam, mu, modes, forces):
    lane = lax.broadcasted_iota(jnp.int32, (8, 128), 1)
    left = lane < 64
    x_up, x_down, y_up, y_down = make_shifts()
    weight = jnp.full((8, 128), table_ref[0, 0] * gl + table_ref[0, 1] * gm, jnp.float32)
    for m in range(1, 4):
        weight = jnp.maximum(weight, table_ref[m, 0] * gl + table_ref[m, 1] * gm)
    step = 1.5 / (1.0 + 8.0 * weight)
    scale = step * (1.0 / 16.0)
    lams = [scale * table_ref[m, 0] for m in range(4)]
    mus = [scale * table_ref[m, 1] for m in range(4)]

    def fetch(row, v):
        even = in_ref[pl.ds(2 * v * SLOT + row, 8, stride=4 * SLOT), :]
        odd = in_ref[pl.ds((2 * v + 1) * SLOT + row, 8, stride=4 * SLOT), :]
        return (
            jnp.where(left, even, pltpu.roll(odd, 64, 1)),
            jnp.where(left, pltpu.roll(even, 64, 1), odd),
        )

    peak = []
    for p in range(WIDE):
        for v in range(2):
            b0, b1 = fetch(p, v)
            b2, ids = fetch(16 + p, v)
            for c, b in enumerate((b0, b1, b2)):
                b = step * b
                u[c, p, v] = b
                u1[c, p, v] = b
            if p < WIDE - 1:
                first, shear = lams[0], mus[0]
                for m in range(1, 4):
                    hit = ids == float(m)
                    first = jnp.where(hit, lams[m], first)
                    shear = jnp.where(hit, mus[m], shear)
                lam[p, v] = first
                mu[p, v] = shear
    for k in range(6):
        for v in range(2):
            near, far = fetch(32 + k, v)
            low[1 + k, v] = near
            low[7 + k, v] = far

    def project(p, v, new, old, own):
        shifted = new if old is None else new + old
        z = jnp.maximum(shifted, low[p, v])
        now = shifted - z
        dual[p, v] = now
        apart = new - z
        quad[p, v] = step * (apart + now)
        if own:
            peak.append(jnp.abs(apart))

    def largest():
        top = peak[0]
        for a in peak[1:]:
            top = jnp.maximum(top, a)
        peak.clear()
        top = jnp.max(top, axis=1, keepdims=True)
        return jnp.max(top, axis=0, keepdims=True)

    mine = range(DEPTH, DEPTH + CHUNK)
    for p in range(1, WIDE - 1):
        for v in range(2):
            project(p, v, u[2, p, v], None, p in mine)
    history = [largest()]
    for t in range(1, ITERS):
        lo, hi = t, WIDE - 1 - t
        for p in range(lo - 1, hi + 2):
            for c in range(3):
                value = (u[c, p, 0], u[c, p, 1])
                other = y_up(value)
                ys, yd = add(other, value), sub(other, value)
                for m, part in ((0, ys), (2, yd)):
                    other = x_up(part)
                    xs, xd = add(other, part), sub(other, part)
                    for v in range(2):
                        modes[c, m, p, v] = xs[v]
                        modes[c, m + 1, p, v] = xd[v]
        for v in range(2):
            held = None
            below = [[modes[c, m, lo - 1, v] for m in range(4)] for c in range(3)]
            for e in range(lo - 1, hi + 1):
                above = [[modes[c, m, e + 1, v] for m in range(4)] for c in range(3)]
                down, up = element(below, above, lam[e, v], mu[e, v])
                if held is not None:
                    for c in range(3):
                        for m in range(4):
                            forces[c, m, e, v] = held[c][m] + down[c][m]
                held, below = up, above
        for p in range(lo, hi + 1):
            for c in range(3):
                f = [(forces[c, m, p, 0], forces[c, m, p, 1]) for m in range(4)]
                ys = add(sub(f[0], f[1]), x_down(add(f[0], f[1])))
                yd = add(sub(f[2], f[3]), x_down(add(f[2], f[3])))
                total = add(sub(ys, yd), y_down(add(ys, yd)))
                for v in range(2):
                    new = u[c, p, v] - total[v] + u1[c, p, v]
                    if c == 2:
                        new = new - quad[p, v]
                        project(p, v, new, dual[p, v], p in mine)
                    u[c, p, v] = new
        history.append(largest())
    gaps = jnp.zeros((8, 128), jnp.float32)
    for t, top in enumerate(history):
        gaps = jnp.where(lane == t, top, gaps)
    for k, p in enumerate(mine):
        for v in range(2):
            for row, a, b in (
                (k, u[0, p, v], u[1, p, v]),
                (CHUNK + k, u[2, p, v], dual[p, v]),
            ):
                even = jnp.where(left, a, pltpu.roll(b, 64, 1))
                odd = jnp.where(left, pltpu.roll(a, 64, 1), b)
                out_ref[pl.ds(2 * v * BACK + row, 8, stride=4 * BACK), :] = even
                out_ref[pl.ds((2 * v + 1) * BACK + row, 8, stride=4 * BACK), :] = odd
    for i in range(4):
        out_ref[pl.ds(i * BACK + 8, 8, stride=4 * BACK), :] = gaps


def bricks_kernel(in_ref, u_ref, w_ref, gaps_ref, rows):
    top = jnp.max(in_ref[:, 8, :], axis=0, keepdims=True)
    gaps_ref[...] = jnp.broadcast_to(top[None], gaps_ref.shape)
    for d in range(32):
        rows[0, CHUNK * d : CHUNK * d + CHUNK] = in_ref[d, 0:CHUNK]
        rows[1, CHUNK * d : CHUNK * d + CHUNK] = in_ref[d, CHUNK : 2 * CHUNK]
    brick = u_ref.shape[1:]
    first = rows[0].T
    u_ref[0] = first[:64].reshape(brick)
    u_ref[1] = first[64:].reshape(brick)
    second = rows[1].T
    u_ref[2] = second[:64].reshape(brick)
    w_ref[0] = jnp.zeros(brick, jnp.float32)
    w_ref[1] = jnp.zeros(brick, jnp.float32)
    w_ref[2] = second[64:].reshape(brick)


def shards(body_load, contact_mask, contact_gap, material_ids, lame_table):
    f32 = jnp.float32
    params = pltpu.CompilerParams(vmem_limit_bytes=32 * 1024 * 1024)
    shape = lambda *dims: jax.ShapeDtypeStruct(dims, f32)
    vmem = pl.BlockSpec(memory_space=pltpu.VMEM)
    smem = pl.BlockSpec(memory_space=pltpu.SMEM)
    rows, first, last = pl.pallas_call(
        turn_kernel,
        out_shape=(shape(3, 128, 128), shape(3, 8, 128), shape(3, 8, 128)),
        in_specs=[vmem] * 4,
        out_specs=(vmem,) * 3,
        compiler_params=params,
        name="turn",
    )(body_load, contact_mask, contact_gap, material_ids)
    count = lax.axis_size("gz")
    before = lax.ppermute(last, "gz", [(i, (i + 1) % count) for i in range(count)])
    after = lax.ppermute(first, "gz", [(i, (i - 1) % count) for i in range(count)])
    slots = pl.pallas_call(
        slots_kernel,
        out_shape=shape(32, SLOT, 128),
        in_specs=[vmem] * 3,
        out_specs=vmem,
        scratch_shapes=[pltpu.VMEM((3, 144, 128), f32)],
        compiler_params=params,
        name="slots",
    )(rows, before, after)
    slots = lax.all_to_all(slots, SWAP, 0, 0, tiled=True)
    gl, gm = bounds()
    back = pl.pallas_call(
        lambda *refs: iterate_kernel(gl, gm, *refs),
        out_shape=shape(32 * BACK, 128),
        in_specs=[smem, vmem],
        out_specs=vmem,
        scratch_shapes=[
            pltpu.VMEM((3, WIDE, 2, 8, 128), f32),
            pltpu.VMEM((3, WIDE, 2, 8, 128), f32),
            pltpu.VMEM((WIDE, 2, 8, 128), f32),
            pltpu.VMEM((WIDE, 2, 8, 128), f32),
            pltpu.VMEM((WIDE, 2, 8, 128), f32),
            pltpu.VMEM((WIDE, 2, 8, 128), f32),
            pltpu.VMEM((WIDE, 2, 8, 128), f32),
            pltpu.VMEM((3, 4, WIDE, 2, 8, 128), f32),
            pltpu.VMEM((3, 4, WIDE, 2, 8, 128), f32),
        ],
        compiler_params=params,
        name="iterate",
    )(lame_table, slots.reshape(32 * SLOT, 128))
    back = lax.all_to_all(back.reshape(32, BACK, 128), SWAP, 0, 0, tiled=True)
    displacement, multiplier, gaps = pl.pallas_call(
        bricks_kernel,
        out_shape=(shape(*body_load.shape), shape(*body_load.shape), shape(count, 8, 128)),
        in_specs=[vmem],
        out_specs=(vmem,) * 3,
        scratch_shapes=[pltpu.VMEM((2, 128, 128), f32)],
        compiler_params=params,
        name="bricks",
    )(back)
    gaps = lax.all_to_all(gaps, "gz", 0, 0, tiled=True)
    return (displacement, multiplier, jnp.max(gaps[:, 0, :ITERS], axis=0))


def solution(mesh):
    node, field = P("gx", "gy", "gz"), P(None, "gx", "gy", "gz")
    return jax.shard_map(
        shards,
        mesh=mesh,
        in_specs=(field, node, node, node, P()),
        out_specs=(field, field, P()),
        check_vma=False,
    )
```

```python
import jax
import jax.numpy as jnp
import numpy as np
from jax import lax
from jax.experimental import pallas as pl
from jax.experimental.pallas import tpu as pltpu
from jax.sharding import PartitionSpec as P

ITERS = 6
DEPTH = ITERS - 1
SWAP = ("gy", "gx")
CHUNK = 4
WIDE = CHUNK + 2 * DEPTH
SLOT = 40
BACK = 16
UNROLL = (7, 4)
GROUPS = (4, 4)
PAD = 0
PLANES = WIDE + max(GROUPS)
LOWEST = float(np.finfo(np.float32).min)


def corner_offsets(a):
    return (a >> 2 & 1, a >> 1 & 1, a & 1)


def element_tables():
    points = np.array([(1.0 - 3.0 ** (-0.5)) / 2.0, (1.0 + 3.0 ** (-0.5)) / 2.0])
    stiff_lame = np.zeros((24, 24))
    stiff_shear = np.zeros((24, 24))
    for p in points:
        for q in points:
            for r in points:
                position = (p, q, r)
                gradients = np.zeros((8, 3))
                for a in range(8):
                    corner = corner_offsets(a)
                    for d in range(3):
                        factor = 1.0
                        for e in range(3):
                            if e == d:
                                factor = factor * (1.0 if corner[e] else -1.0)
                            else:
                                factor = factor * (position[e] if corner[e] else 1.0 - position[e])
                        gradients[a, d] = factor
                for a in range(8):
                    for c in range(3):
                        for b in range(8):
                            for d in range(3):
                                stiff_lame[3 * a + c, 3 * b + d] += (
                                    0.125 * gradients[a, c] * gradients[b, d]
                                )
                                stiff_shear[3 * a + c, 3 * b + d] += 0.125 * (
                                    float(c == d) * np.dot(gradients[a], gradients[b])
                                    + gradients[a, d] * gradients[b, c]
                                )
    return (stiff_lame, stiff_shear)


def bounds():
    stiff_lame, stiff_shear = element_tables()
    return (
        float(np.max(np.sum(np.abs(stiff_lame), 1))),
        float(np.max(np.sum(np.abs(stiff_shear), 1))),
    )


def turn_kernel(load_ref, mask_ref, gap_ref, ids_ref, rows_ref, first_ref, last_ref):
    flat = lambda v: v.reshape(64, 128)
    low = jnp.where(mask_ref[...] > 0, -gap_ref[...], LOWEST)
    low = flat(low)
    ids = flat(ids_ref[...].astype(jnp.float32))
    pairs = (
        (flat(load_ref[0]), flat(load_ref[1])),
        (flat(load_ref[2]), ids),
        (low, low),
    )
    for i, pair in enumerate(pairs):
        turned = jnp.concatenate(pair, 0).T
        rows_ref[i] = turned
        first_ref[i] = turned[:8]
        last_ref[i] = turned[120:]


def slots_kernel(rows_ref, before_ref, after_ref, out_ref, wide):
    for i in range(3):
        wide[i, 0:8] = before_ref[i]
        wide[i, 8:136] = rows_ref[i]
        wide[i, 136:144] = after_ref[i]
    lower = lax.broadcasted_iota(jnp.int32, (6, 128), 1) < 64
    for d in range(32):
        at = CHUNK * d + 8 - DEPTH
        out_ref[d, 0:WIDE] = wide[0, at : at + WIDE]
        out_ref[d, 16 : 16 + WIDE] = wide[1, at : at + WIDE]
        out_ref[d, 32:38] = jnp.where(
            lower, wide[2, at + 1 : at + 7], wide[2, at + 7 : at + 13]
        )


def flip(v, even):
    return jnp.where(even, pltpu.roll(v, 7, 0), pltpu.roll(v, 1, 0))


def make_shifts():
    lane = lax.broadcasted_iota(jnp.int32, (8, 128), 1)
    even = lax.broadcasted_iota(jnp.int32, (8, 128), 0) % 2 == 0
    top_x, low_x = lane >= 112, lane < 16
    top_y, low_y = lane % 16 == 15, lane % 16 == 0

    def x_up(v):
        r0, r1 = pltpu.roll(v[0], 112, 1), pltpu.roll(v[1], 112, 1)
        return (jnp.where(top_x, r1, r0), jnp.where(top_x, flip(r0, even), r1))

    def x_down(v):
        r0, r1 = pltpu.roll(v[0], 16, 1), pltpu.roll(v[1], 16, 1)
        return (jnp.where(low_x, flip(r1, even), r0), jnp.where(low_x, r0, r1))

    def y_up(v):
        return tuple(
            jnp.where(top_y, pltpu.roll(pltpu.roll(a, 6, 0), 15, 1), pltpu.roll(a, 127, 1))
            for a in v
        )

    def y_down(v):
        return tuple(
            jnp.where(low_y, pltpu.roll(pltpu.roll(a, 2, 0), 113, 1), pltpu.roll(a, 1, 1))
            for a in v
        )

    return (x_up, x_down, y_up, y_down)


def add(a, b):
    return tuple(i + j for i, j in zip(a, b))


def sub(a, b):
    return tuple(i - j for i, j in zip(a, b))


def element(low, high, lam, mu):
    s = [[h + l for l, h in zip(low[c], high[c])] for c in range(3)]
    d = [[h - l for l, h in zip(low[c], high[c])] for c in range(3)]
    lam3, mu3, mu2 = lam * (1.0 / 3.0), mu * (1.0 / 3.0), mu + mu
    last = (lam + 4.0 * mu) * (1.0 / 9.0)
    SS, DS, SD, DD = range(4)
    fs = [[None] * 4 for _ in range(3)]
    fd = [[None] * 4 for _ in range(3)]
    exx, eyy, ezz = s[0][DS], s[1][SD], d[2][SS]
    trace = lam * (exx + eyy + ezz)
    fs[0][DS] = trace + mu2 * exx
    fs[1][SD] = trace + mu2 * eyy
    fd[2][SS] = trace + mu2 * ezz
    fs[0][SD] = fs[1][DS] = mu * (s[0][SD] + s[1][DS])
    fd[0][SS] = fs[2][DS] = mu * (d[0][SS] + s[2][DS])
    fd[1][SS] = fs[2][SD] = mu * (d[1][SS] + s[2][SD])
    both = lam3 * (s[0][DD] + d[2][SD])
    fs[0][DD] = both + mu * s[0][DD]
    fd[2][SD] = both + mu * d[2][SD]
    both = lam3 * (s[1][DD] + d[2][DS])
    fs[1][DD] = both + mu * s[1][DD]
    fd[2][DS] = both + mu * d[2][DS]
    both = lam3 * (d[0][DS] + d[1][SD])
    fd[0][DS] = both + mu * d[0][DS]
    fd[1][SD] = both + mu * d[1][SD]
    total = s[2][DD] + d[1][DS] + d[0][SD]
    fs[2][DD] = mu3 * (total + s[2][DD])
    fd[1][DS] = mu3 * (total + d[1][DS])
    fd[0][SD] = mu3 * (total + d[0][SD])
    for c in range(3):
        fd[c][DD] = last * d[c][DD]
    down = [[-fd[c][0]] + [fs[c][m] - fd[c][m] for m in (1, 2, 3)] for c in range(3)]
    up = [[fd[c][0]] + [fs[c][m] + fd[c][m] for m in (1, 2, 3)] for c in range(3)]
    return (down, up)


def loop(lo, hi, body, unroll):
    lax.fori_loop(lo, hi, lambda i, _: body(i), None, unroll=unroll)


def planes(lo, hi, group, body):
    def step(g, _):
        for j in range(group):
            body(lo + g * group + j)

    lax.fori_loop(0, -(-(hi - lo) // group), step, None)


def iterate_kernel(gl, gm, table_ref, in_ref, out_ref, u, u1, quad, dual, dist, low, lam, mu, modes, forces):
    lane = lax.broadcasted_iota(jnp.int32, (8, 128), 1)
    left = lane < 64
    x_up, x_down, y_up, y_down = make_shifts()
    weight = jnp.full((8, 128), table_ref[0, 0] * gl + table_ref[0, 1] * gm, jnp.float32)
    for m in range(1, 4):
        weight = jnp.maximum(weight, table_ref[m, 0] * gl + table_ref[m, 1] * gm)
    step = 1.5 / (1.0 + 8.0 * weight)
    scale = step * (1.0 / 16.0)
    lams = [scale * table_ref[m, 0] for m in range(4)]
    mus = [scale * table_ref[m, 1] for m in range(4)]

    def fetch(row, v):
        even = in_ref[pl.ds(2 * v * SLOT + row, 8, stride=4 * SLOT), :]
        odd = in_ref[pl.ds((2 * v + 1) * SLOT + row, 8, stride=4 * SLOT), :]
        return (
            jnp.where(left, even, pltpu.roll(odd, 64, 1)),
            jnp.where(left, pltpu.roll(even, 64, 1), odd),
        )

    def unpack(k):
        p = PAD + k
        for v in range(2):
            b0, b1 = fetch(k, v)
            b2, ids = fetch(16 + k, v)
            for c, b in enumerate((b0, b1, b2)):
                b = step * b
                u[c, p, v] = b
                u1[c, p, v] = b
            first, shear = lams[0], mus[0]
            for m in range(1, 4):
                hit = ids == float(m)
                first = jnp.where(hit, lams[m], first)
                shear = jnp.where(hit, mus[m], shear)
            lam[p, v] = first
            mu[p, v] = shear

    loop(0, WIDE, unpack, UNROLL[0])
    for k in range(6):
        for v in range(2):
            near, far = fetch(32 + k, v)
            low[PAD + 1 + k, v] = near
            low[PAD + 7 + k, v] = far

    def project(new, old, bound):
        shifted = new if old is None else add(new, old)
        z = tuple(jnp.maximum(a, b) for a, b in zip(shifted, bound))
        now, apart = sub(shifted, z), sub(new, z)
        return (now, tuple(step * a for a in add(apart, now)), tuple(jnp.abs(a) for a in apart))

    def keep(p, results):
        for ref, value in zip((dual, quad, dist), results):
            put(ref, value, p)

    def largest():
        top = dist[mine[0], 0]
        for p in mine:
            for v in range(2):
                top = jnp.maximum(top, dist[p, v])
        return top

    def pair(ref, *at):
        return tuple(ref[*at, v] for v in range(2))

    def put(ref, value, *at):
        for v in range(2):
            ref[*at, v] = value[v]

    def split(value, shift):
        other = shift(value)
        return (add(other, value), sub(other, value))

    def forward(p):
        for c in range(3):
            for m, part in enumerate(split(pair(u, c, p), y_up)):
                for k, value in enumerate(split(part, x_up)):
                    put(modes, value, c, 2 * m + k, p)

    def layer(v):
        def body(e, carry):
            held, below = carry
            above = [[modes[c, m, e + 1, v] for m in range(4)] for c in range(3)]
            down, up = element(below, above, lam[e, v], mu[e, v])
            for c in range(3):
                for m in range(4):
                    forces[c, m, e, v] = held[c][m] + down[c][m]
            return (up, above)

        return body

    def first_project(p):
        keep(p, project(pair(u, 2, p), None, pair(low, p)))

    def merge(s, d, shift):
        return add(sub(s, d), shift(add(s, d)))

    def backward(p):
        for c in range(3):
            f = [pair(forces, c, m, p) for m in range(4)]
            total = merge(merge(f[0], f[1], x_down), merge(f[2], f[3], x_down), y_down)
            new = add(sub(pair(u, c, p), total), pair(u1, c, p))
            if c == 2:
                new = sub(new, pair(quad, p))
                keep(p, project(new, pair(dual, p), pair(low, p)))
            put(u, new, c, p)

    mine = range(PAD + DEPTH, PAD + DEPTH + CHUNK)
    loop(PAD + 1, PAD + WIDE - 1, first_project, UNROLL[0])
    history = [largest()]
    zero = jnp.zeros((8, 128), jnp.float32)
    for t in range(1, ITERS):
        lo, hi = PAD + t, PAD + WIDE - 1 - t
        planes(lo - 1, hi + 2, GROUPS[0], forward)
        for v in range(2):
            below = [[modes[c, m, lo - 1, v] for m in range(4)] for c in range(3)]
            held = [[zero] * 4 for _ in range(3)]
            lax.fori_loop(lo - 1, hi + 1, layer(v), (held, below), unroll=UNROLL[1])
        planes(lo, hi + 1, GROUPS[1], backward)
        history.append(largest())
    gaps = jnp.zeros((8, 128), jnp.float32)
    for t, top in enumerate(history):
        top = jnp.max(jnp.max(top, axis=0, keepdims=True), axis=1, keepdims=True)
        gaps = jnp.where(lane == t, top, gaps)
    for k, p in enumerate(mine):
        for v in range(2):
            for row, a, b in (
                (k, u[0, p, v], u[1, p, v]),
                (CHUNK + k, u[2, p, v], dual[p, v]),
            ):
                even = jnp.where(left, a, pltpu.roll(b, 64, 1))
                odd = jnp.where(left, pltpu.roll(a, 64, 1), b)
                out_ref[pl.ds(2 * v * BACK + row, 8, stride=4 * BACK), :] = even
                out_ref[pl.ds((2 * v + 1) * BACK + row, 8, stride=4 * BACK), :] = odd
    for i in range(4):
        out_ref[pl.ds(i * BACK + 8, 8, stride=4 * BACK), :] = gaps


def bricks_kernel(in_ref, u_ref, w_ref, gaps_ref, rows):
    top = jnp.max(in_ref[:, 8, :], axis=0, keepdims=True)
    gaps_ref[...] = jnp.broadcast_to(top[None], gaps_ref.shape)
    for d in range(32):
        rows[0, CHUNK * d : CHUNK * d + CHUNK] = in_ref[d, 0:CHUNK]
        rows[1, CHUNK * d : CHUNK * d + CHUNK] = in_ref[d, CHUNK : 2 * CHUNK]
    brick = u_ref.shape[1:]
    first = rows[0].T
    u_ref[0] = first[:64].reshape(brick)
    u_ref[1] = first[64:].reshape(brick)
    second = rows[1].T
    u_ref[2] = second[:64].reshape(brick)
    w_ref[0] = jnp.zeros(brick, jnp.float32)
    w_ref[1] = jnp.zeros(brick, jnp.float32)
    w_ref[2] = second[64:].reshape(brick)


def shards(body_load, contact_mask, contact_gap, material_ids, lame_table):
    f32 = jnp.float32
    params = pltpu.CompilerParams(vmem_limit_bytes=32 * 1024 * 1024)
    shape = lambda *dims: jax.ShapeDtypeStruct(dims, f32)
    vmem = pl.BlockSpec(memory_space=pltpu.VMEM)
    smem = pl.BlockSpec(memory_space=pltpu.SMEM)
    rows, first, last = pl.pallas_call(
        turn_kernel,
        out_shape=(shape(3, 128, 128), shape(3, 8, 128), shape(3, 8, 128)),
        in_specs=[vmem] * 4,
        out_specs=(vmem,) * 3,
        compiler_params=params,
        name="turn",
    )(body_load, contact_mask, contact_gap, material_ids)
    count = lax.axis_size("gz")
    before = lax.ppermute(last, "gz", [(i, (i + 1) % count) for i in range(count)])
    after = lax.ppermute(first, "gz", [(i, (i - 1) % count) for i in range(count)])
    slots = pl.pallas_call(
        slots_kernel,
        out_shape=shape(32, SLOT, 128),
        in_specs=[vmem] * 3,
        out_specs=vmem,
        scratch_shapes=[pltpu.VMEM((3, 144, 128), f32)],
        compiler_params=params,
        name="slots",
    )(rows, before, after)
    slots = lax.all_to_all(slots, SWAP, 0, 0, tiled=True)
    gl, gm = bounds()
    back = pl.pallas_call(
        lambda *refs: iterate_kernel(gl, gm, *refs),
        out_shape=shape(32 * BACK, 128),
        in_specs=[smem, vmem],
        out_specs=vmem,
        scratch_shapes=[
            pltpu.VMEM((3, PLANES, 2, 8, 128), f32),
            pltpu.VMEM((3, PLANES, 2, 8, 128), f32),
            pltpu.VMEM((PLANES, 2, 8, 128), f32),
            pltpu.VMEM((PLANES, 2, 8, 128), f32),
            pltpu.VMEM((PLANES, 2, 8, 128), f32),
            pltpu.VMEM((PLANES, 2, 8, 128), f32),
            pltpu.VMEM((PLANES, 2, 8, 128), f32),
            pltpu.VMEM((PLANES, 2, 8, 128), f32),
            pltpu.VMEM((3, 4, PLANES, 2, 8, 128), f32),
            pltpu.VMEM((3, 4, PLANES, 2, 8, 128), f32),
        ],
        compiler_params=params,
        name="iterate",
    )(lame_table, slots.reshape(32 * SLOT, 128))
    back = lax.all_to_all(back.reshape(32, BACK, 128), SWAP, 0, 0, tiled=True)
    displacement, multiplier, gaps = pl.pallas_call(
        bricks_kernel,
        out_shape=(shape(*body_load.shape), shape(*body_load.shape), shape(count, 8, 128)),
        in_specs=[vmem],
        out_specs=(vmem,) * 3,
        scratch_shapes=[pltpu.VMEM((2, 128, 128), f32)],
        compiler_params=params,
        name="bricks",
    )(back)
    gaps = lax.all_to_all(gaps, "gz", 0, 0, tiled=True)
    return (displacement, multiplier, jnp.max(gaps[:, 0, :ITERS], axis=0))


def solution(mesh):
    node, field = P("gx", "gy", "gz"), P(None, "gx", "gy", "gz")
    return jax.shard_map(
        shards,
        mesh=mesh,
        in_specs=(field, node, node, node, P()),
        out_specs=(field, field, P()),
        check_vma=False,
    )
```

```python
import jax
import jax.numpy as jnp
import numpy as np
from jax import lax
from jax.experimental import pallas as pl
from jax.experimental.pallas import tpu as pltpu
from jax.sharding import PartitionSpec as P

ITERS = 6
DEPTH = ITERS - 1
SWAP = ("gy", "gx")
CHUNK = 4
WIDE = CHUNK + 2 * DEPTH
SLOT = 34
BACK = 9
UNROLL = (7, 4)
GROUPS = (4, 4)
PAD = 0
PLANES = WIDE + max(GROUPS)
LOWEST = float(np.finfo(np.float32).min)


def corner_offsets(a):
    return (a >> 2 & 1, a >> 1 & 1, a & 1)


def element_tables():
    points = np.array([(1.0 - 3.0 ** (-0.5)) / 2.0, (1.0 + 3.0 ** (-0.5)) / 2.0])
    stiff_lame = np.zeros((24, 24))
    stiff_shear = np.zeros((24, 24))
    for p in points:
        for q in points:
            for r in points:
                position = (p, q, r)
                gradients = np.zeros((8, 3))
                for a in range(8):
                    corner = corner_offsets(a)
                    for d in range(3):
                        factor = 1.0
                        for e in range(3):
                            if e == d:
                                factor = factor * (1.0 if corner[e] else -1.0)
                            else:
                                factor = factor * (position[e] if corner[e] else 1.0 - position[e])
                        gradients[a, d] = factor
                for a in range(8):
                    for c in range(3):
                        for b in range(8):
                            for d in range(3):
                                stiff_lame[3 * a + c, 3 * b + d] += (
                                    0.125 * gradients[a, c] * gradients[b, d]
                                )
                                stiff_shear[3 * a + c, 3 * b + d] += 0.125 * (
                                    float(c == d) * np.dot(gradients[a], gradients[b])
                                    + gradients[a, d] * gradients[b, c]
                                )
    return (stiff_lame, stiff_shear)


def bounds():
    stiff_lame, stiff_shear = element_tables()
    return (
        float(np.max(np.sum(np.abs(stiff_lame), 1))),
        float(np.max(np.sum(np.abs(stiff_shear), 1))),
    )


def turn_kernel(*refs):
    inputs, (rows_ref, first_ref, last_ref), scratch, sems = refs[:4], refs[4:7], refs[7:11], refs[11]
    copies = [
        pltpu.make_async_copy(source, target, sems.at[i])
        for i, (source, target) in enumerate(zip(inputs, scratch))
    ]
    for copy in copies:
        copy.start()
    for copy in copies:
        copy.wait()
    load_ref, mask_ref, gap_ref, ids_ref = scratch
    flat = lambda v: v.reshape(64, 128)
    low = flat(jnp.where(mask_ref[...] > 0, -gap_ref[...], LOWEST))
    ids = flat(ids_ref[...].astype(jnp.float32))
    pairs = (
        (flat(load_ref[0]), flat(load_ref[1])),
        (flat(load_ref[2]), ids),
        (low, low),
    )
    for i, pair in enumerate(pairs):
        turned = jnp.concatenate(pair, 0).T
        rows_ref[i] = turned
        first_ref[i] = turned[:8]
        last_ref[i] = turned[120:]


def slots_kernel(rows_ref, before_ref, after_ref, out_ref, wide):
    for i in range(3):
        wide[i, 0:8] = before_ref[i]
        wide[i, 8:136] = rows_ref[i]
        wide[i, 136:144] = after_ref[i]
    lower = lax.broadcasted_iota(jnp.int32, (6, 128), 1) < 64
    for d in range(32):
        at = CHUNK * d + 8 - DEPTH
        to = SLOT * d
        out_ref[to : to + WIDE] = wide[0, at : at + WIDE]
        out_ref[to + WIDE : to + 2 * WIDE] = wide[1, at : at + WIDE]
        out_ref[to + 2 * WIDE : to + SLOT] = jnp.where(
            lower, wide[2, at + 1 : at + 7], wide[2, at + 7 : at + 13]
        )


def flip(v, even):
    return jnp.where(even, pltpu.roll(v, 7, 0), pltpu.roll(v, 1, 0))


def make_shifts():
    lane = lax.broadcasted_iota(jnp.int32, (8, 128), 1)
    even = lax.broadcasted_iota(jnp.int32, (8, 128), 0) % 2 == 0
    top_x, low_x = lane >= 112, lane < 16
    top_y, low_y = lane % 16 == 15, lane % 16 == 0

    def x_up(v):
        r0, r1 = pltpu.roll(v[0], 112, 1), pltpu.roll(v[1], 112, 1)
        return (jnp.where(top_x, r1, r0), jnp.where(top_x, flip(r0, even), r1))

    def x_down(v):
        r0, r1 = pltpu.roll(v[0], 16, 1), pltpu.roll(v[1], 16, 1)
        return (jnp.where(low_x, flip(r1, even), r0), jnp.where(low_x, r0, r1))

    def y_up(v):
        return tuple(
            jnp.where(top_y, pltpu.roll(pltpu.roll(a, 6, 0), 15, 1), pltpu.roll(a, 127, 1))
            for a in v
        )

    def y_down(v):
        return tuple(
            jnp.where(low_y, pltpu.roll(pltpu.roll(a, 2, 0), 113, 1), pltpu.roll(a, 1, 1))
            for a in v
        )

    return (x_up, x_down, y_up, y_down)


def add(a, b):
    return tuple(i + j for i, j in zip(a, b))


def sub(a, b):
    return tuple(i - j for i, j in zip(a, b))


def element(low, high, lam, mu):
    s = [[h + l for l, h in zip(low[c], high[c])] for c in range(3)]
    d = [[h - l for l, h in zip(low[c], high[c])] for c in range(3)]
    lam3, mu3, mu2 = lam * (1.0 / 3.0), mu * (1.0 / 3.0), mu + mu
    last = (lam + 4.0 * mu) * (1.0 / 9.0)
    SS, DS, SD, DD = range(4)
    fs = [[None] * 4 for _ in range(3)]
    fd = [[None] * 4 for _ in range(3)]
    exx, eyy, ezz = s[0][DS], s[1][SD], d[2][SS]
    trace = lam * (exx + eyy + ezz)
    fs[0][DS] = trace + mu2 * exx
    fs[1][SD] = trace + mu2 * eyy
    fd[2][SS] = trace + mu2 * ezz
    fs[0][SD] = fs[1][DS] = mu * (s[0][SD] + s[1][DS])
    fd[0][SS] = fs[2][DS] = mu * (d[0][SS] + s[2][DS])
    fd[1][SS] = fs[2][SD] = mu * (d[1][SS] + s[2][SD])
    both = lam3 * (s[0][DD] + d[2][SD])
    fs[0][DD] = both + mu * s[0][DD]
    fd[2][SD] = both + mu * d[2][SD]
    both = lam3 * (s[1][DD] + d[2][DS])
    fs[1][DD] = both + mu * s[1][DD]
    fd[2][DS] = both + mu * d[2][DS]
    both = lam3 * (d[0][DS] + d[1][SD])
    fd[0][DS] = both + mu * d[0][DS]
    fd[1][SD] = both + mu * d[1][SD]
    total = s[2][DD] + d[1][DS] + d[0][SD]
    fs[2][DD] = mu3 * (total + s[2][DD])
    fd[1][DS] = mu3 * (total + d[1][DS])
    fd[0][SD] = mu3 * (total + d[0][SD])
    for c in range(3):
        fd[c][DD] = last * d[c][DD]
    down = [[-fd[c][0]] + [fs[c][m] - fd[c][m] for m in (1, 2, 3)] for c in range(3)]
    up = [[fd[c][0]] + [fs[c][m] + fd[c][m] for m in (1, 2, 3)] for c in range(3)]
    return (down, up)


def loop(lo, hi, body, unroll):
    lax.fori_loop(lo, hi, lambda i, _: body(i), None, unroll=unroll)


def planes(lo, hi, group, body):
    def step(g, _):
        for j in range(group):
            body(lo + g * group + j)

    lax.fori_loop(0, -(-(hi - lo) // group), step, None)


def iterate_kernel(gl, gm, table_ref, in_ref, out_ref, u, u1, quad, dual, dist, low, lam, mu, modes, forces):
    lane = lax.broadcasted_iota(jnp.int32, (8, 128), 1)
    left = lane < 64
    x_up, x_down, y_up, y_down = make_shifts()
    weight = jnp.full((8, 128), table_ref[0, 0] * gl + table_ref[0, 1] * gm, jnp.float32)
    for m in range(1, 4):
        weight = jnp.maximum(weight, table_ref[m, 0] * gl + table_ref[m, 1] * gm)
    step = 1.5 / (1.0 + 8.0 * weight)
    scale = step * (1.0 / 16.0)
    lams = [scale * table_ref[m, 0] for m in range(4)]
    mus = [scale * table_ref[m, 1] for m in range(4)]

    def fetch(row, v):
        even = in_ref[pl.ds(2 * v * SLOT + row, 8, stride=4 * SLOT), :]
        odd = in_ref[pl.ds((2 * v + 1) * SLOT + row, 8, stride=4 * SLOT), :]
        return (
            jnp.where(left, even, pltpu.roll(odd, 64, 1)),
            jnp.where(left, pltpu.roll(even, 64, 1), odd),
        )

    def unpack(k):
        p = PAD + k
        for v in range(2):
            b0, b1 = fetch(k, v)
            b2, ids = fetch(WIDE + k, v)
            for c, b in enumerate((b0, b1, b2)):
                b = step * b
                u[c, p, v] = b
                u1[c, p, v] = b
            first, shear = lams[0], mus[0]
            for m in range(1, 4):
                hit = ids == float(m)
                first = jnp.where(hit, lams[m], first)
                shear = jnp.where(hit, mus[m], shear)
            lam[p, v] = first
            mu[p, v] = shear

    loop(0, WIDE, unpack, UNROLL[0])
    for k in range(6):
        for v in range(2):
            near, far = fetch(2 * WIDE + k, v)
            low[PAD + 1 + k, v] = near
            low[PAD + 7 + k, v] = far

    def project(new, old, bound):
        shifted = new if old is None else add(new, old)
        z = tuple(jnp.maximum(a, b) for a, b in zip(shifted, bound))
        now, apart = sub(shifted, z), sub(new, z)
        return (now, tuple(step * a for a in add(apart, now)), tuple(jnp.abs(a) for a in apart))

    def keep(p, results):
        for ref, value in zip((dual, quad, dist), results):
            put(ref, value, p)

    def largest():
        top = dist[mine[0], 0]
        for p in mine:
            for v in range(2):
                top = jnp.maximum(top, dist[p, v])
        return top

    def pair(ref, *at):
        return tuple(ref[*at, v] for v in range(2))

    def put(ref, value, *at):
        for v in range(2):
            ref[*at, v] = value[v]

    def split(value, shift):
        other = shift(value)
        return (add(other, value), sub(other, value))

    def forward(p):
        for c in range(3):
            for m, part in enumerate(split(pair(u, c, p), y_up)):
                for k, value in enumerate(split(part, x_up)):
                    put(modes, value, c, 2 * m + k, p)

    def layer(v):
        def body(e, carry):
            held, below = carry
            above = [[modes[c, m, e + 1, v] for m in range(4)] for c in range(3)]
            down, up = element(below, above, lam[e, v], mu[e, v])
            for c in range(3):
                for m in range(4):
                    forces[c, m, e, v] = held[c][m] + down[c][m]
            return (up, above)

        return body

    def first_project(p):
        keep(p, project(pair(u, 2, p), None, pair(low, p)))

    def merge(s, d, shift):
        return add(sub(s, d), shift(add(s, d)))

    def backward(p):
        for c in range(3):
            f = [pair(forces, c, m, p) for m in range(4)]
            total = merge(merge(f[0], f[1], x_down), merge(f[2], f[3], x_down), y_down)
            new = add(sub(pair(u, c, p), total), pair(u1, c, p))
            if c == 2:
                new = sub(new, pair(quad, p))
                keep(p, project(new, pair(dual, p), pair(low, p)))
            put(u, new, c, p)

    mine = range(PAD + DEPTH, PAD + DEPTH + CHUNK)
    loop(PAD + 1, PAD + WIDE - 1, first_project, UNROLL[0])
    history = [largest()]
    zero = jnp.zeros((8, 128), jnp.float32)
    for t in range(1, ITERS):
        lo, hi = PAD + t, PAD + WIDE - 1 - t
        planes(lo - 1, hi + 2, GROUPS[0], forward)
        for v in range(2):
            below = [[modes[c, m, lo - 1, v] for m in range(4)] for c in range(3)]
            held = [[zero] * 4 for _ in range(3)]
            lax.fori_loop(lo - 1, hi + 1, layer(v), (held, below), unroll=UNROLL[1])
        planes(lo, hi + 1, GROUPS[1], backward)
        history.append(largest())
    gaps = jnp.zeros((8, 128), jnp.float32)
    for t, top in enumerate(history):
        top = jnp.max(jnp.max(top, axis=0, keepdims=True), axis=1, keepdims=True)
        gaps = jnp.where(lane == t, top, gaps)
    for k, p in enumerate(mine):
        for v in range(2):
            for row, a, b in (
                (k, u[0, p, v], u[1, p, v]),
                (CHUNK + k, u[2, p, v], dual[p, v]),
            ):
                even = jnp.where(left, a, pltpu.roll(b, 64, 1))
                odd = jnp.where(left, pltpu.roll(a, 64, 1), b)
                out_ref[pl.ds(2 * v * BACK + row, 8, stride=4 * BACK), :] = even
                out_ref[pl.ds((2 * v + 1) * BACK + row, 8, stride=4 * BACK), :] = odd
    for i in range(4):
        out_ref[pl.ds(i * BACK + 8, 8, stride=4 * BACK), :] = gaps


def bricks_kernel(in_ref, u_ref, w_ref, gaps_ref, rows):
    top = in_ref[pl.ds(2 * CHUNK, 32, stride=BACK), :]
    top = jnp.max(top, axis=0, keepdims=True)
    gaps_ref[...] = jnp.broadcast_to(top[None], gaps_ref.shape)
    for d in range(32):
        for i in range(2):
            at = BACK * d + CHUNK * i
            rows[i, CHUNK * d : CHUNK * d + CHUNK] = in_ref[at : at + CHUNK]
    brick = u_ref.shape[1:]
    first = rows[0].T
    u_ref[0] = first[:64].reshape(brick)
    u_ref[1] = first[64:].reshape(brick)
    second = rows[1].T
    u_ref[2] = second[:64].reshape(brick)
    w_ref[0] = jnp.zeros(brick, jnp.float32)
    w_ref[1] = jnp.zeros(brick, jnp.float32)
    w_ref[2] = second[64:].reshape(brick)


def swap(rows, each):
    thin = 2 if each % 2 == 0 else 1
    parts = rows.reshape(32, each // thin, thin, 128)
    return lax.all_to_all(parts, SWAP, 0, 0, tiled=True).reshape(rows.shape)


def shards(body_load, contact_mask, contact_gap, material_ids, lame_table):
    f32 = jnp.float32
    params = pltpu.CompilerParams(vmem_limit_bytes=32 * 1024 * 1024)
    whole = pltpu.CompilerParams(vmem_limit_bytes=60 * 1024 * 1024)
    shape = lambda *dims: jax.ShapeDtypeStruct(dims, f32)
    vmem = pl.BlockSpec(memory_space=pltpu.VMEM)
    smem = pl.BlockSpec(memory_space=pltpu.SMEM)
    inputs = (body_load, contact_mask, contact_gap, material_ids)
    rows, first, last = pl.pallas_call(
        turn_kernel,
        out_shape=(shape(3, 128, 128), shape(3, 8, 128), shape(3, 8, 128)),
        in_specs=[pl.BlockSpec(memory_space=pltpu.HBM)] * 4,
        out_specs=(vmem,) * 3,
        scratch_shapes=[pltpu.VMEM(a.shape, a.dtype) for a in inputs]
        + [pltpu.SemaphoreType.DMA((4,))],
        compiler_params=whole,
        name="turn",
    )(*inputs)
    count = lax.axis_size("gz")
    before = lax.ppermute(last, "gz", [(i, (i + 1) % count) for i in range(count)])
    after = lax.ppermute(first, "gz", [(i, (i - 1) % count) for i in range(count)])
    slots = pl.pallas_call(
        slots_kernel,
        out_shape=shape(32 * SLOT, 128),
        in_specs=[vmem] * 3,
        out_specs=vmem,
        scratch_shapes=[pltpu.VMEM((3, 144, 128), f32)],
        compiler_params=params,
        name="slots",
    )(rows, before, after)
    slots = swap(slots, SLOT)
    gl, gm = bounds()
    back = pl.pallas_call(
        lambda *refs: iterate_kernel(gl, gm, *refs),
        out_shape=shape(32 * BACK, 128),
        in_specs=[smem, vmem],
        out_specs=vmem,
        scratch_shapes=[
            pltpu.VMEM((3, PLANES, 2, 8, 128), f32),
            pltpu.VMEM((3, PLANES, 2, 8, 128), f32),
            pltpu.VMEM((PLANES, 2, 8, 128), f32),
            pltpu.VMEM((PLANES, 2, 8, 128), f32),
            pltpu.VMEM((PLANES, 2, 8, 128), f32),
            pltpu.VMEM((PLANES, 2, 8, 128), f32),
            pltpu.VMEM((PLANES, 2, 8, 128), f32),
            pltpu.VMEM((PLANES, 2, 8, 128), f32),
            pltpu.VMEM((3, 4, PLANES, 2, 8, 128), f32),
            pltpu.VMEM((3, 4, PLANES, 2, 8, 128), f32),
        ],
        compiler_params=params,
        name="iterate",
    )(lame_table, slots)
    back = swap(back, BACK)
    displacement, multiplier, gaps = pl.pallas_call(
        bricks_kernel,
        out_shape=(shape(*body_load.shape), shape(*body_load.shape), shape(count, 8, 128)),
        in_specs=[vmem],
        out_specs=(vmem,) * 3,
        scratch_shapes=[pltpu.VMEM((2, 128, 128), f32)],
        compiler_params=params,
        name="bricks",
    )(back)
    gaps = lax.all_to_all(gaps, "gz", 0, 0, tiled=True)
    return (displacement, multiplier, jnp.max(gaps[:, 0, :ITERS], axis=0))


def solution(mesh):
    node, field = P("gx", "gy", "gz"), P(None, "gx", "gy", "gz")
    return jax.shard_map(
        shards,
        mesh=mesh,
        in_specs=(field, node, node, node, P()),
        out_specs=(field, field, P()),
        check_vma=False,
    )
```

```python
import jax
import jax.numpy as jnp
import numpy as np
from jax import lax
from jax.experimental import pallas as pl
from jax.experimental.pallas import tpu as pltpu
from jax.sharding import PartitionSpec as P

ITERS = 6
DEPTH = ITERS - 1
SWAP = ("gy", "gx")
CHUNK = 4
WIDE = CHUNK + 2 * DEPTH
SLOT = 34
BACK = 9
EDGE = 4
UNROLL = (14, 13)
GROUPS = (WIDE, WIDE - 2, WIDE, WIDE - 2)
PAD = 0
PLANES = WIDE + max(GROUPS)
LOWEST = float(np.finfo(np.float32).min)


def corner_offsets(a):
    return (a >> 2 & 1, a >> 1 & 1, a & 1)


def element_tables():
    points = np.array([(1.0 - 3.0 ** (-0.5)) / 2.0, (1.0 + 3.0 ** (-0.5)) / 2.0])
    stiff_lame = np.zeros((24, 24))
    stiff_shear = np.zeros((24, 24))
    for p in points:
        for q in points:
            for r in points:
                position = (p, q, r)
                gradients = np.zeros((8, 3))
                for a in range(8):
                    corner = corner_offsets(a)
                    for d in range(3):
                        factor = 1.0
                        for e in range(3):
                            if e == d:
                                factor = factor * (1.0 if corner[e] else -1.0)
                            else:
                                factor = factor * (position[e] if corner[e] else 1.0 - position[e])
                        gradients[a, d] = factor
                for a in range(8):
                    for c in range(3):
                        for b in range(8):
                            for d in range(3):
                                stiff_lame[3 * a + c, 3 * b + d] += (
                                    0.125 * gradients[a, c] * gradients[b, d]
                                )
                                stiff_shear[3 * a + c, 3 * b + d] += 0.125 * (
                                    float(c == d) * np.dot(gradients[a], gradients[b])
                                    + gradients[a, d] * gradients[b, c]
                                )
    return (stiff_lame, stiff_shear)


def bounds():
    stiff_lame, stiff_shear = element_tables()
    return (
        float(np.max(np.sum(np.abs(stiff_lame), 1))),
        float(np.max(np.sum(np.abs(stiff_shear), 1))),
    )


def turn_kernel(*refs):
    inputs, (rows_ref, first_ref, last_ref), scratch, sems = refs[:4], refs[4:7], refs[7:11], refs[11]
    copies = [
        pltpu.make_async_copy(source, target, sems.at[i])
        for i, (source, target) in enumerate(zip(inputs, scratch))
    ]
    for copy in copies:
        copy.start()
    for copy in copies:
        copy.wait()
    load_ref, mask_ref, gap_ref, ids_ref = scratch
    flat = lambda v: v.reshape(64, 128)
    low = flat(jnp.where(mask_ref[...] > 0, -gap_ref[...], LOWEST))
    ids = flat(ids_ref[...].astype(jnp.float32))
    pairs = (
        (flat(load_ref[0]), flat(load_ref[1])),
        (flat(load_ref[2]), ids),
        (low, low),
    )
    for i, pair in enumerate(pairs):
        turned = jnp.concatenate(pair, 0).T
        rows_ref[i] = turned
        first_ref[i] = turned[:8]
        last_ref[i] = turned[120:]


def fill(out_ref, wide, first, begin, end, to):
    lower = lax.broadcasted_iota(jnp.int32, (6, 128), 1) < 64
    for d in range(begin, end):
        at = CHUNK * d - DEPTH - first
        row = SLOT * d - to
        out_ref[row : row + WIDE] = wide[0, at : at + WIDE]
        out_ref[row + WIDE : row + 2 * WIDE] = wide[1, at : at + WIDE]
        out_ref[row + 2 * WIDE : row + SLOT] = jnp.where(
            lower, wide[2, at + 1 : at + 7], wide[2, at + 7 : at + 13]
        )


def inner_kernel(rows_ref, out_ref):
    fill(out_ref, rows_ref, 0, EDGE, 32 - EDGE, 0)


def outer_kernel(rows_ref, before_ref, after_ref, _, out_ref, wide, part, sems):
    for i in range(3):
        wide[0, i, 0:8] = before_ref[i]
        wide[0, i, 8:32] = rows_ref[i, 0:24]
        wide[1, i, 0:24] = rows_ref[i, 104:128]
        wide[1, i, 24:32] = after_ref[i]
    copies = []
    for side, begin, first in ((0, 0, -8), (1, 32 - EDGE, 104)):
        fill(part.at[side], wide.at[side], first, begin, begin + EDGE, SLOT * begin)
        target = out_ref.at[pl.ds(SLOT * begin, SLOT * EDGE)]
        copies.append(pltpu.make_async_copy(part.at[side], target, sems.at[side]))
        copies[-1].start()
    for copy in copies:
        copy.wait()


def flip(v, even):
    return jnp.where(even, pltpu.roll(v, 7, 0), pltpu.roll(v, 1, 0))


def make_shifts():
    lane = lax.broadcasted_iota(jnp.int32, (8, 128), 1)
    even = lax.broadcasted_iota(jnp.int32, (8, 128), 0) % 2 == 0
    top_x, low_x = lane >= 112, lane < 16
    top_y, low_y = lane % 16 == 15, lane % 16 == 0

    def x_up(v):
        r0, r1 = pltpu.roll(v[0], 112, 1), pltpu.roll(v[1], 112, 1)
        return (jnp.where(top_x, r1, r0), jnp.where(top_x, flip(r0, even), r1))

    def x_down(v):
        r0, r1 = pltpu.roll(v[0], 16, 1), pltpu.roll(v[1], 16, 1)
        return (jnp.where(low_x, flip(r1, even), r0), jnp.where(low_x, r0, r1))

    def y_up(v):
        return tuple(
            jnp.where(top_y, pltpu.roll(pltpu.roll(a, 6, 0), 15, 1), pltpu.roll(a, 127, 1))
            for a in v
        )

    def y_down(v):
        return tuple(
            jnp.where(low_y, pltpu.roll(pltpu.roll(a, 2, 0), 113, 1), pltpu.roll(a, 1, 1))
            for a in v
        )

    return (x_up, x_down, y_up, y_down)


def add(a, b):
    return tuple(i + j for i, j in zip(a, b))


def sub(a, b):
    return tuple(i - j for i, j in zip(a, b))


def element(low, high, lam, mu):
    s = [[h + l for l, h in zip(low[c], high[c])] for c in range(3)]
    d = [[h - l for l, h in zip(low[c], high[c])] for c in range(3)]
    lam3, mu3, mu2 = lam * (1.0 / 3.0), mu * (1.0 / 3.0), mu + mu
    last = (lam + 4.0 * mu) * (1.0 / 9.0)
    SS, DS, SD, DD = range(4)
    fs = [[None] * 4 for _ in range(3)]
    fd = [[None] * 4 for _ in range(3)]
    exx, eyy, ezz = s[0][DS], s[1][SD], d[2][SS]
    trace = lam * (exx + eyy + ezz)
    fs[0][DS] = trace + mu2 * exx
    fs[1][SD] = trace + mu2 * eyy
    fd[2][SS] = trace + mu2 * ezz
    fs[0][SD] = fs[1][DS] = mu * (s[0][SD] + s[1][DS])
    fd[0][SS] = fs[2][DS] = mu * (d[0][SS] + s[2][DS])
    fd[1][SS] = fs[2][SD] = mu * (d[1][SS] + s[2][SD])
    both = lam3 * (s[0][DD] + d[2][SD])
    fs[0][DD] = both + mu * s[0][DD]
    fd[2][SD] = both + mu * d[2][SD]
    both = lam3 * (s[1][DD] + d[2][DS])
    fs[1][DD] = both + mu * s[1][DD]
    fd[2][DS] = both + mu * d[2][DS]
    both = lam3 * (d[0][DS] + d[1][SD])
    fd[0][DS] = both + mu * d[0][DS]
    fd[1][SD] = both + mu * d[1][SD]
    total = s[2][DD] + d[1][DS] + d[0][SD]
    fs[2][DD] = mu3 * (total + s[2][DD])
    fd[1][DS] = mu3 * (total + d[1][DS])
    fd[0][SD] = mu3 * (total + d[0][SD])
    for c in range(3):
        fd[c][DD] = last * d[c][DD]
    down = [[-fd[c][0]] + [fs[c][m] - fd[c][m] for m in (1, 2, 3)] for c in range(3)]
    up = [[fd[c][0]] + [fs[c][m] + fd[c][m] for m in (1, 2, 3)] for c in range(3)]
    return (down, up)


def loop(lo, hi, body, unroll):
    lax.fori_loop(lo, hi, lambda i, _: body(i), None, unroll=unroll)


def planes(lo, hi, group, body):
    group = min(group, hi - lo)

    def step(g, _):
        for j in range(group):
            body(lo + g * group + j)

    lax.fori_loop(0, -(-(hi - lo) // group), step, None)


def iterate_kernel(gl, gm, table_ref, in_ref, out_ref, u, u1, quad, dual, dist, low, lam, mu, halfway, modes, forces):
    lane = lax.broadcasted_iota(jnp.int32, (8, 128), 1)
    left = lane < 64
    x_up, x_down, y_up, y_down = make_shifts()
    weight = jnp.full((8, 128), table_ref[0, 0] * gl + table_ref[0, 1] * gm, jnp.float32)
    for m in range(1, 4):
        weight = jnp.maximum(weight, table_ref[m, 0] * gl + table_ref[m, 1] * gm)
    step = 1.5 / (1.0 + 8.0 * weight)
    scale = step * (1.0 / 16.0)
    lams = [scale * table_ref[m, 0] for m in range(4)]
    mus = [scale * table_ref[m, 1] for m in range(4)]

    def fetch(row, v):
        even = in_ref[pl.ds(2 * v * SLOT + row, 8, stride=4 * SLOT), :]
        odd = in_ref[pl.ds((2 * v + 1) * SLOT + row, 8, stride=4 * SLOT), :]
        return (
            jnp.where(left, even, pltpu.roll(odd, 64, 1)),
            jnp.where(left, pltpu.roll(even, 64, 1), odd),
        )

    def unpack(k):
        p = PAD + k
        for v in range(2):
            b0, b1 = fetch(k, v)
            b2, ids = fetch(WIDE + k, v)
            for c, b in enumerate((b0, b1, b2)):
                b = step * b
                u[c, p, v] = b
                u1[c, p, v] = b
            first, shear = lams[0], mus[0]
            for m in range(1, 4):
                hit = ids == float(m)
                first = jnp.where(hit, lams[m], first)
                shear = jnp.where(hit, mus[m], shear)
            lam[p, v] = first
            mu[p, v] = shear

    loop(0, WIDE, unpack, UNROLL[0])
    for k in range(6):
        for v in range(2):
            near, far = fetch(2 * WIDE + k, v)
            low[PAD + 1 + k, v] = near
            low[PAD + 7 + k, v] = far

    def project(new, old, bound):
        shifted = new if old is None else add(new, old)
        z = tuple(jnp.maximum(a, b) for a, b in zip(shifted, bound))
        now, apart = sub(shifted, z), sub(new, z)
        return (now, tuple(step * a for a in add(apart, now)), tuple(jnp.abs(a) for a in apart))

    def keep(p, results):
        for ref, value in zip((dual, quad, dist), results):
            put(ref, value, p)

    def largest():
        top = dist[mine[0], 0]
        for p in mine:
            for v in range(2):
                top = jnp.maximum(top, dist[p, v])
        return top

    def pair(ref, *at):
        return tuple(ref[*at, v] for v in range(2))

    def put(ref, value, *at):
        for v in range(2):
            ref[*at, v] = value[v]

    def split(value, shift):
        other = shift(value)
        return (add(other, value), sub(other, value))

    def forward_y(p):
        for c in range(3):
            for m, part in enumerate(split(pair(u, c, p), y_up)):
                put(halfway, part, c, m, p)

    def forward_x(p):
        for c in range(3):
            for m in range(2):
                for k, value in enumerate(split(pair(halfway, c, m, p), x_up)):
                    put(modes, value, c, 2 * m + k, p)

    def layer(v):
        def body(e, carry):
            held, below = carry
            above = [[modes[c, m, e + 1, v] for m in range(4)] for c in range(3)]
            down, up = element(below, above, lam[e, v], mu[e, v])
            for c in range(3):
                for m in range(4):
                    forces[c, m, e, v] = held[c][m] + down[c][m]
            return (up, above)

        return body

    def first_project(p):
        keep(p, project(pair(u, 2, p), None, pair(low, p)))

    def merge(s, d, shift):
        return add(sub(s, d), shift(add(s, d)))

    def backward_x(p):
        for c in range(3):
            f = [pair(forces, c, m, p) for m in range(4)]
            ys, yd = merge(f[0], f[1], x_down), merge(f[2], f[3], x_down)
            put(halfway, sub(ys, yd), c, 0, p)
            put(halfway, add(ys, yd), c, 1, p)

    def backward_y(p):
        for c in range(3):
            total = add(pair(halfway, c, 0, p), y_down(pair(halfway, c, 1, p)))
            new = add(sub(pair(u, c, p), total), pair(u1, c, p))
            if c == 2:
                new = sub(new, pair(quad, p))
                keep(p, project(new, pair(dual, p), pair(low, p)))
            put(u, new, c, p)

    mine = range(PAD + DEPTH, PAD + DEPTH + CHUNK)
    loop(PAD + 1, PAD + WIDE - 1, first_project, UNROLL[0])
    history = [largest()]
    zero = jnp.zeros((8, 128), jnp.float32)
    for t in range(1, ITERS):
        lo, hi = PAD + t, PAD + WIDE - 1 - t
        planes(lo - 1, hi + 2, GROUPS[0], forward_y)
        planes(lo - 1, hi + 2, GROUPS[2], forward_x)
        for v in range(2):
            below = [[modes[c, m, lo - 1, v] for m in range(4)] for c in range(3)]
            held = [[zero] * 4 for _ in range(3)]
            lax.fori_loop(lo - 1, hi + 1, layer(v), (held, below), unroll=min(UNROLL[1], hi + 2 - lo))
        planes(lo, hi + 1, GROUPS[1], backward_x)
        planes(lo, hi + 1, GROUPS[3], backward_y)
        history.append(largest())
    gaps = jnp.zeros((8, 128), jnp.float32)
    for t, top in enumerate(history):
        top = jnp.max(jnp.max(top, axis=0, keepdims=True), axis=1, keepdims=True)
        gaps = jnp.where(lane == t, top, gaps)
    for k, p in enumerate(mine):
        for v in range(2):
            for row, a, b in (
                (k, u[0, p, v], u[1, p, v]),
                (CHUNK + k, u[2, p, v], dual[p, v]),
            ):
                even = jnp.where(left, a, pltpu.roll(b, 64, 1))
                odd = jnp.where(left, pltpu.roll(a, 64, 1), b)
                out_ref[pl.ds(2 * v * BACK + row, 8, stride=4 * BACK), :] = even
                out_ref[pl.ds((2 * v + 1) * BACK + row, 8, stride=4 * BACK), :] = odd
    for i in range(4):
        out_ref[pl.ds(i * BACK + 8, 8, stride=4 * BACK), :] = gaps


def gaps_kernel(in_ref, gaps_ref):
    top = in_ref[pl.ds(2 * CHUNK, 32, stride=BACK), :]
    top = jnp.max(top, axis=0, keepdims=True)
    gaps_ref[...] = jnp.broadcast_to(top[None], gaps_ref.shape)


def bricks_kernel(in_ref, u_ref, w_ref, rows):
    for d in range(32):
        for i in range(2):
            at = BACK * d + CHUNK * i
            rows[i, CHUNK * d : CHUNK * d + CHUNK] = in_ref[at : at + CHUNK]
    brick = u_ref.shape[1:]
    first = rows[0].T
    u_ref[0] = first[:64].reshape(brick)
    u_ref[1] = first[64:].reshape(brick)
    second = rows[1].T
    u_ref[2] = second[:64].reshape(brick)
    w_ref[0] = jnp.zeros(brick, jnp.float32)
    w_ref[1] = jnp.zeros(brick, jnp.float32)
    w_ref[2] = second[64:].reshape(brick)


def swap(rows, each):
    thin = 2 if each % 2 == 0 else 1
    parts = rows.reshape(32, each // thin, thin, 128)
    return lax.all_to_all(parts, SWAP, 0, 0, tiled=True).reshape(rows.shape)


def shards(body_load, contact_mask, contact_gap, material_ids, lame_table):
    f32 = jnp.float32
    params = pltpu.CompilerParams(vmem_limit_bytes=32 * 1024 * 1024)
    whole = pltpu.CompilerParams(vmem_limit_bytes=60 * 1024 * 1024)
    shape = lambda *dims: jax.ShapeDtypeStruct(dims, f32)
    vmem = pl.BlockSpec(memory_space=pltpu.VMEM)
    smem = pl.BlockSpec(memory_space=pltpu.SMEM)
    hbm = pl.BlockSpec(memory_space=pltpu.HBM)
    inputs = (body_load, contact_mask, contact_gap, material_ids)
    rows, first, last = pl.pallas_call(
        turn_kernel,
        out_shape=(shape(3, 128, 128), shape(3, 8, 128), shape(3, 8, 128)),
        in_specs=[hbm] * 4,
        out_specs=(vmem,) * 3,
        scratch_shapes=[pltpu.VMEM(a.shape, a.dtype) for a in inputs]
        + [pltpu.SemaphoreType.DMA((4,))],
        compiler_params=whole,
        name="turn",
    )(*inputs)
    count = lax.axis_size("gz")
    before = lax.ppermute(last, "gz", [(i, (i + 1) % count) for i in range(count)])
    after = lax.ppermute(first, "gz", [(i, (i - 1) % count) for i in range(count)])
    slots = pl.pallas_call(
        inner_kernel,
        out_shape=shape(32 * SLOT, 128),
        in_specs=[vmem],
        out_specs=vmem,
        compiler_params=params,
        cost_estimate=pl.CostEstimate(flops=0, bytes_accessed=1 << 22, transcendentals=0),
        name="inner",
    )(rows)
    slots = pl.pallas_call(
        outer_kernel,
        out_shape=shape(32 * SLOT, 128),
        in_specs=[vmem] * 3 + [hbm],
        out_specs=hbm,
        scratch_shapes=[
            pltpu.VMEM((2, 3, 32, 128), f32),
            pltpu.VMEM((2, SLOT * EDGE, 128), f32),
            pltpu.SemaphoreType.DMA((2,)),
        ],
        input_output_aliases={3: 0},
        compiler_params=params,
        name="outer",
    )(rows, before, after, slots)
    slots = swap(slots, SLOT)
    gl, gm = bounds()
    back = pl.pallas_call(
        lambda *refs: iterate_kernel(gl, gm, *refs),
        out_shape=shape(32 * BACK, 128),
        in_specs=[smem, vmem],
        out_specs=vmem,
        scratch_shapes=[
            pltpu.VMEM((3, PLANES, 2, 8, 128), f32),
            pltpu.VMEM((3, PLANES, 2, 8, 128), f32),
            pltpu.VMEM((PLANES, 2, 8, 128), f32),
            pltpu.VMEM((PLANES, 2, 8, 128), f32),
            pltpu.VMEM((PLANES, 2, 8, 128), f32),
            pltpu.VMEM((PLANES, 2, 8, 128), f32),
            pltpu.VMEM((PLANES, 2, 8, 128), f32),
            pltpu.VMEM((PLANES, 2, 8, 128), f32),
            pltpu.VMEM((3, 2, PLANES, 2, 8, 128), f32),
            pltpu.VMEM((3, 4, PLANES, 2, 8, 128), f32),
            pltpu.VMEM((3, 4, PLANES, 2, 8, 128), f32),
        ],
        compiler_params=params,
        name="iterate",
    )(lame_table, slots)
    back = swap(back, BACK)
    gaps = pl.pallas_call(
        gaps_kernel,
        out_shape=shape(count, 1, 128),
        in_specs=[vmem],
        out_specs=vmem,
        compiler_params=params,
        name="gaps",
    )(back)
    displacement, multiplier = pl.pallas_call(
        bricks_kernel,
        out_shape=(shape(*body_load.shape), shape(*body_load.shape)),
        in_specs=[vmem],
        out_specs=(vmem,) * 2,
        scratch_shapes=[pltpu.VMEM((2, 128, 128), f32)],
        compiler_params=params,
        cost_estimate=pl.CostEstimate(flops=0, bytes_accessed=1 << 22, transcendentals=0),
        name="bricks",
    )(back)
    gaps = lax.all_to_all(gaps, "gz", 0, 0, tiled=True)
    return (displacement, multiplier, jnp.max(gaps[:, 0, :ITERS], axis=0))


def solution(mesh):
    node, field = P("gx", "gy", "gz"), P(None, "gx", "gy", "gz")
    return jax.shard_map(
        shards,
        mesh=mesh,
        in_specs=(field, node, node, node, P()),
        out_specs=(field, field, P()),
        check_vma=False,
    )
```

```python
import jax
import jax.numpy as jnp
import numpy as np
from jax import lax
from jax.experimental import pallas as pl
from jax.experimental.pallas import tpu as pltpu
from jax.sharding import PartitionSpec as P

ITERS = 6
DEPTH = ITERS - 1
SWAP = ("gy", "gx")
CHUNK = 4
WIDE = CHUNK + 2 * DEPTH
SLOT = 34
BACK = 9
EDGE = 4
UNROLL = (14, 13)
GROUPS = (WIDE, WIDE - 2, WIDE, WIDE - 2)
PAD = 0
PLANES = WIDE + max(GROUPS)
LOWEST = float(np.finfo(np.float32).min)


def corner_offsets(a):
    return (a >> 2 & 1, a >> 1 & 1, a & 1)


def element_tables():
    points = np.array([(1.0 - 3.0 ** (-0.5)) / 2.0, (1.0 + 3.0 ** (-0.5)) / 2.0])
    stiff_lame = np.zeros((24, 24))
    stiff_shear = np.zeros((24, 24))
    for p in points:
        for q in points:
            for r in points:
                position = (p, q, r)
                gradients = np.zeros((8, 3))
                for a in range(8):
                    corner = corner_offsets(a)
                    for d in range(3):
                        factor = 1.0
                        for e in range(3):
                            if e == d:
                                factor = factor * (1.0 if corner[e] else -1.0)
                            else:
                                factor = factor * (position[e] if corner[e] else 1.0 - position[e])
                        gradients[a, d] = factor
                for a in range(8):
                    for c in range(3):
                        for b in range(8):
                            for d in range(3):
                                stiff_lame[3 * a + c, 3 * b + d] += (
                                    0.125 * gradients[a, c] * gradients[b, d]
                                )
                                stiff_shear[3 * a + c, 3 * b + d] += 0.125 * (
                                    float(c == d) * np.dot(gradients[a], gradients[b])
                                    + gradients[a, d] * gradients[b, c]
                                )
    return (stiff_lame, stiff_shear)


def bounds():
    stiff_lame, stiff_shear = element_tables()
    return (
        float(np.max(np.sum(np.abs(stiff_lame), 1))),
        float(np.max(np.sum(np.abs(stiff_shear), 1))),
    )


def turn_kernel(*refs):
    load, mask, gap, ids, rows_ref, first_ref, last_ref = refs[:7]
    load_ref, mask_ref, gap_ref, ids_ref, turned, in_sems, out_sems = refs[7:]
    pieces = [(load.at[i], load_ref.at[i]) for i in range(3)]
    pieces += [(mask, mask_ref), (gap, gap_ref), (ids, ids_ref)]
    incoming = [pltpu.make_async_copy(*piece, in_sems.at[i]) for i, piece in enumerate(pieces)]
    for copy in incoming:
        copy.start()
    for copy in incoming:
        copy.wait()
    flat = lambda v: v.reshape(64, 128)
    low = flat(jnp.where(mask_ref[...] > 0, -gap_ref[...], LOWEST))
    ids = flat(ids_ref[...].astype(jnp.float32))
    pairs = (
        (flat(load_ref[0]), flat(load_ref[1])),
        (flat(load_ref[2]), ids),
        (low, low),
    )
    outgoing = []
    for i, pair in enumerate(pairs):
        turned[i] = jnp.concatenate(pair, 0).T
        for k, (source, target) in enumerate(
            (
                (turned.at[i], rows_ref.at[i]),
                (turned.at[i, pl.ds(0, 8)], first_ref.at[i]),
                (turned.at[i, pl.ds(120, 8)], last_ref.at[i]),
            )
        ):
            outgoing.append(pltpu.make_async_copy(source, target, out_sems.at[i, k]))
            outgoing[-1].start()
    for copy in outgoing:
        copy.wait()


def fill(out_ref, wide, first, begin, end, to):
    lower = lax.broadcasted_iota(jnp.int32, (6, 128), 1) < 64
    for d in range(begin, end):
        at = CHUNK * d - DEPTH - first
        row = SLOT * d - to
        out_ref[row : row + WIDE] = wide[0, at : at + WIDE]
        out_ref[row + WIDE : row + 2 * WIDE] = wide[1, at : at + WIDE]
        out_ref[row + 2 * WIDE : row + SLOT] = jnp.where(
            lower, wide[2, at + 1 : at + 7], wide[2, at + 7 : at + 13]
        )


def inner_kernel(rows_ref, out_ref, part, sems):
    copies = []
    for side in range(32 // EDGE - 2):
        begin = EDGE * (side + 1)
        fill(part.at[side], rows_ref, 0, begin, begin + EDGE, SLOT * begin)
        target = out_ref.at[pl.ds(SLOT * begin, SLOT * EDGE)]
        copies.append(pltpu.make_async_copy(part.at[side], target, sems.at[side]))
        copies[-1].start()
    for copy in copies:
        copy.wait()


def outer_kernel(rows_ref, before_ref, after_ref, _, out_ref, wide, part, sems):
    for i in range(3):
        wide[0, i, 0:8] = before_ref[i]
        wide[0, i, 8:32] = rows_ref[i, 0:24]
        wide[1, i, 0:24] = rows_ref[i, 104:128]
        wide[1, i, 24:32] = after_ref[i]
    copies = []
    for side, begin, first in ((0, 0, -8), (1, 32 - EDGE, 104)):
        fill(part.at[side], wide.at[side], first, begin, begin + EDGE, SLOT * begin)
        target = out_ref.at[pl.ds(SLOT * begin, SLOT * EDGE)]
        copies.append(pltpu.make_async_copy(part.at[side], target, sems.at[side]))
        copies[-1].start()
    for copy in copies:
        copy.wait()


def flip(v, even):
    return jnp.where(even, pltpu.roll(v, 7, 0), pltpu.roll(v, 1, 0))


def make_shifts():
    lane = lax.broadcasted_iota(jnp.int32, (8, 128), 1)
    even = lax.broadcasted_iota(jnp.int32, (8, 128), 0) % 2 == 0
    top_x, low_x = lane >= 112, lane < 16
    top_y, low_y = lane % 16 == 15, lane % 16 == 0

    def x_up(v):
        r0, r1 = pltpu.roll(v[0], 112, 1), pltpu.roll(v[1], 112, 1)
        return (jnp.where(top_x, r1, r0), jnp.where(top_x, flip(r0, even), r1))

    def x_down(v):
        r0, r1 = pltpu.roll(v[0], 16, 1), pltpu.roll(v[1], 16, 1)
        return (jnp.where(low_x, flip(r1, even), r0), jnp.where(low_x, r0, r1))

    def y_up(v):
        return tuple(
            jnp.where(top_y, pltpu.roll(pltpu.roll(a, 6, 0), 15, 1), pltpu.roll(a, 127, 1))
            for a in v
        )

    def y_down(v):
        return tuple(
            jnp.where(low_y, pltpu.roll(pltpu.roll(a, 2, 0), 113, 1), pltpu.roll(a, 1, 1))
            for a in v
        )

    return (x_up, x_down, y_up, y_down)


def add(a, b):
    return tuple(i + j for i, j in zip(a, b))


def sub(a, b):
    return tuple(i - j for i, j in zip(a, b))


def element(low, high, lam, mu):
    s = [[h + l for l, h in zip(low[c], high[c])] for c in range(3)]
    d = [[h - l for l, h in zip(low[c], high[c])] for c in range(3)]
    lam3, mu3, mu2 = lam * (1.0 / 3.0), mu * (1.0 / 3.0), mu + mu
    last = (lam + 4.0 * mu) * (1.0 / 9.0)
    SS, DS, SD, DD = range(4)
    fs = [[None] * 4 for _ in range(3)]
    fd = [[None] * 4 for _ in range(3)]
    exx, eyy, ezz = s[0][DS], s[1][SD], d[2][SS]
    trace = lam * (exx + eyy + ezz)
    fs[0][DS] = trace + mu2 * exx
    fs[1][SD] = trace + mu2 * eyy
    fd[2][SS] = trace + mu2 * ezz
    fs[0][SD] = fs[1][DS] = mu * (s[0][SD] + s[1][DS])
    fd[0][SS] = fs[2][DS] = mu * (d[0][SS] + s[2][DS])
    fd[1][SS] = fs[2][SD] = mu * (d[1][SS] + s[2][SD])
    both = lam3 * (s[0][DD] + d[2][SD])
    fs[0][DD] = both + mu * s[0][DD]
    fd[2][SD] = both + mu * d[2][SD]
    both = lam3 * (s[1][DD] + d[2][DS])
    fs[1][DD] = both + mu * s[1][DD]
    fd[2][DS] = both + mu * d[2][DS]
    both = lam3 * (d[0][DS] + d[1][SD])
    fd[0][DS] = both + mu * d[0][DS]
    fd[1][SD] = both + mu * d[1][SD]
    total = s[2][DD] + d[1][DS] + d[0][SD]
    fs[2][DD] = mu3 * (total + s[2][DD])
    fd[1][DS] = mu3 * (total + d[1][DS])
    fd[0][SD] = mu3 * (total + d[0][SD])
    for c in range(3):
        fd[c][DD] = last * d[c][DD]
    down = [[-fd[c][0]] + [fs[c][m] - fd[c][m] for m in (1, 2, 3)] for c in range(3)]
    up = [[fd[c][0]] + [fs[c][m] + fd[c][m] for m in (1, 2, 3)] for c in range(3)]
    return (down, up)


def loop(lo, hi, body, unroll):
    lax.fori_loop(lo, hi, lambda i, _: body(i), None, unroll=unroll)


def planes(lo, hi, group, body):
    group = min(group, hi - lo)

    def step(g, _):
        for j in range(group):
            body(lo + g * group + j)

    lax.fori_loop(0, -(-(hi - lo) // group), step, None)


def iterate_kernel(gl, gm, table_ref, in_ref, out_ref, u, u1, quad, dual, dist, low, lam, mu, halfway, modes, forces):
    lane = lax.broadcasted_iota(jnp.int32, (8, 128), 1)
    left = lane < 64
    x_up, x_down, y_up, y_down = make_shifts()
    weight = jnp.full((8, 128), table_ref[0, 0] * gl + table_ref[0, 1] * gm, jnp.float32)
    for m in range(1, 4):
        weight = jnp.maximum(weight, table_ref[m, 0] * gl + table_ref[m, 1] * gm)
    step = 1.5 / (1.0 + 8.0 * weight)
    scale = step * (1.0 / 16.0)
    lams = [scale * table_ref[m, 0] for m in range(4)]
    mus = [scale * table_ref[m, 1] for m in range(4)]

    def fetch(row, v):
        even = in_ref[pl.ds(2 * v * SLOT + row, 8, stride=4 * SLOT), :]
        odd = in_ref[pl.ds((2 * v + 1) * SLOT + row, 8, stride=4 * SLOT), :]
        return (
            jnp.where(left, even, pltpu.roll(odd, 64, 1)),
            jnp.where(left, pltpu.roll(even, 64, 1), odd),
        )

    def unpack(k):
        p = PAD + k
        for v in range(2):
            b0, b1 = fetch(k, v)
            b2, ids = fetch(WIDE + k, v)
            for c, b in enumerate((b0, b1, b2)):
                b = step * b
                u[c, p, v] = b
                u1[c, p, v] = b
            first, shear = lams[0], mus[0]
            for m in range(1, 4):
                hit = ids == float(m)
                first = jnp.where(hit, lams[m], first)
                shear = jnp.where(hit, mus[m], shear)
            lam[p, v] = first
            mu[p, v] = shear

    loop(0, WIDE, unpack, UNROLL[0])
    for k in range(6):
        for v in range(2):
            near, far = fetch(2 * WIDE + k, v)
            low[PAD + 1 + k, v] = near
            low[PAD + 7 + k, v] = far

    def project(new, old, bound):
        shifted = new if old is None else add(new, old)
        z = tuple(jnp.maximum(a, b) for a, b in zip(shifted, bound))
        now, apart = sub(shifted, z), sub(new, z)
        return (now, tuple(step * a for a in add(apart, now)), tuple(jnp.abs(a) for a in apart))

    def keep(p, results):
        for ref, value in zip((dual, quad, dist), results):
            put(ref, value, p)

    def largest():
        top = dist[mine[0], 0]
        for p in mine:
            for v in range(2):
                top = jnp.maximum(top, dist[p, v])
        return top

    def pair(ref, *at):
        return tuple(ref[*at, v] for v in range(2))

    def put(ref, value, *at):
        for v in range(2):
            ref[*at, v] = value[v]

    def split(value, shift):
        other = shift(value)
        return (add(other, value), sub(other, value))

    def forward_y(p):
        for c in range(3):
            for m, part in enumerate(split(pair(u, c, p), y_up)):
                put(halfway, part, c, m, p)

    def forward_x(p):
        for c in range(3):
            for m in range(2):
                for k, value in enumerate(split(pair(halfway, c, m, p), x_up)):
                    put(modes, value, c, 2 * m + k, p)

    def layer(v):
        def body(e, carry):
            held, below = carry
            above = [[modes[c, m, e + 1, v] for m in range(4)] for c in range(3)]
            down, up = element(below, above, lam[e, v], mu[e, v])
            for c in range(3):
                for m in range(4):
                    forces[c, m, e, v] = held[c][m] + down[c][m]
            return (up, above)

        return body

    def first_project(p):
        keep(p, project(pair(u, 2, p), None, pair(low, p)))

    def merge(s, d, shift):
        return add(sub(s, d), shift(add(s, d)))

    def backward_x(p):
        for c in range(3):
            f = [pair(forces, c, m, p) for m in range(4)]
            ys, yd = merge(f[0], f[1], x_down), merge(f[2], f[3], x_down)
            put(halfway, sub(ys, yd), c, 0, p)
            put(halfway, add(ys, yd), c, 1, p)

    def backward_y(p):
        for c in range(3):
            total = add(pair(halfway, c, 0, p), y_down(pair(halfway, c, 1, p)))
            new = add(sub(pair(u, c, p), total), pair(u1, c, p))
            if c == 2:
                new = sub(new, pair(quad, p))
                keep(p, project(new, pair(dual, p), pair(low, p)))
            put(u, new, c, p)

    mine = range(PAD + DEPTH, PAD + DEPTH + CHUNK)
    loop(PAD + 1, PAD + WIDE - 1, first_project, UNROLL[0])
    history = [largest()]
    zero = jnp.zeros((8, 128), jnp.float32)
    for t in range(1, ITERS):
        lo, hi = PAD + t, PAD + WIDE - 1 - t
        planes(lo - 1, hi + 2, GROUPS[0], forward_y)
        planes(lo - 1, hi + 2, GROUPS[2], forward_x)
        for v in range(2):
            below = [[modes[c, m, lo - 1, v] for m in range(4)] for c in range(3)]
            held = [[zero] * 4 for _ in range(3)]
            lax.fori_loop(lo - 1, hi + 1, layer(v), (held, below), unroll=min(UNROLL[1], hi + 2 - lo))
        planes(lo, hi + 1, GROUPS[1], backward_x)
        planes(lo, hi + 1, GROUPS[3], backward_y)
        history.append(largest())
    gaps = jnp.zeros((8, 128), jnp.float32)
    for t, top in enumerate(history):
        top = jnp.max(jnp.max(top, axis=0, keepdims=True), axis=1, keepdims=True)
        gaps = jnp.where(lane == t, top, gaps)
    for k, p in enumerate(mine):
        for v in range(2):
            for row, a, b in (
                (k, u[0, p, v], u[1, p, v]),
                (CHUNK + k, u[2, p, v], dual[p, v]),
            ):
                even = jnp.where(left, a, pltpu.roll(b, 64, 1))
                odd = jnp.where(left, pltpu.roll(a, 64, 1), b)
                out_ref[pl.ds(2 * v * BACK + row, 8, stride=4 * BACK), :] = even
                out_ref[pl.ds((2 * v + 1) * BACK + row, 8, stride=4 * BACK), :] = odd
    for i in range(4):
        out_ref[pl.ds(i * BACK + 8, 8, stride=4 * BACK), :] = gaps


def gaps_kernel(in_ref, gaps_ref):
    top = in_ref[pl.ds(2 * CHUNK, 32, stride=BACK), :]
    top = jnp.max(top, axis=0, keepdims=True)
    gaps_ref[...] = jnp.broadcast_to(top[None], gaps_ref.shape)


def bricks_kernel(in_ref, u_ref, w_ref, rows):
    for d in range(32):
        for i in range(2):
            at = BACK * d + CHUNK * i
            rows[i, CHUNK * d : CHUNK * d + CHUNK] = in_ref[at : at + CHUNK]
    brick = u_ref.shape[1:]
    first = rows[0].T
    u_ref[0] = first[:64].reshape(brick)
    u_ref[1] = first[64:].reshape(brick)
    second = rows[1].T
    u_ref[2] = second[:64].reshape(brick)
    w_ref[0] = jnp.zeros(brick, jnp.float32)
    w_ref[1] = jnp.zeros(brick, jnp.float32)
    w_ref[2] = second[64:].reshape(brick)


def swap(rows, each):
    thin = 2 if each % 2 == 0 else 1
    parts = rows.reshape(32, each // thin, thin, 128)
    return lax.all_to_all(parts, SWAP, 0, 0, tiled=True).reshape(rows.shape)


def shards(body_load, contact_mask, contact_gap, material_ids, lame_table):
    f32 = jnp.float32
    params = pltpu.CompilerParams(vmem_limit_bytes=32 * 1024 * 1024)
    whole = pltpu.CompilerParams(vmem_limit_bytes=60 * 1024 * 1024)
    shape = lambda *dims: jax.ShapeDtypeStruct(dims, f32)
    vmem = pl.BlockSpec(memory_space=pltpu.VMEM)
    smem = pl.BlockSpec(memory_space=pltpu.SMEM)
    hbm = pl.BlockSpec(memory_space=pltpu.HBM)
    inputs = (body_load, contact_mask, contact_gap, material_ids)
    rows, first, last = pl.pallas_call(
        turn_kernel,
        out_shape=(shape(3, 128, 128), shape(3, 8, 128), shape(3, 8, 128)),
        in_specs=[hbm] * 4,
        out_specs=(hbm,) * 3,
        scratch_shapes=[pltpu.VMEM(a.shape, a.dtype) for a in inputs]
        + [
            pltpu.VMEM((3, 128, 128), f32),
            pltpu.SemaphoreType.DMA((6,)),
            pltpu.SemaphoreType.DMA((3, 3)),
        ],
        compiler_params=whole,
        name="turn",
    )(*inputs)
    count = lax.axis_size("gz")
    before = lax.ppermute(last, "gz", [(i, (i + 1) % count) for i in range(count)])
    after = lax.ppermute(first, "gz", [(i, (i - 1) % count) for i in range(count)])
    slots = pl.pallas_call(
        inner_kernel,
        out_shape=shape(32 * SLOT, 128),
        in_specs=[vmem],
        out_specs=hbm,
        scratch_shapes=[
            pltpu.VMEM((32 // EDGE - 2, SLOT * EDGE, 128), f32),
            pltpu.SemaphoreType.DMA((32 // EDGE - 2,)),
        ],
        compiler_params=params,
        cost_estimate=pl.CostEstimate(flops=0, bytes_accessed=1 << 22, transcendentals=0),
        name="inner",
    )(rows)
    slots = pl.pallas_call(
        outer_kernel,
        out_shape=shape(32 * SLOT, 128),
        in_specs=[vmem] * 3 + [hbm],
        out_specs=hbm,
        scratch_shapes=[
            pltpu.VMEM((2, 3, 32, 128), f32),
            pltpu.VMEM((2, SLOT * EDGE, 128), f32),
            pltpu.SemaphoreType.DMA((2,)),
        ],
        input_output_aliases={3: 0},
        compiler_params=params,
        name="outer",
    )(rows, before, after, slots)
    slots = swap(slots, SLOT)
    gl, gm = bounds()
    back = pl.pallas_call(
        lambda *refs: iterate_kernel(gl, gm, *refs),
        out_shape=shape(32 * BACK, 128),
        in_specs=[smem, vmem],
        out_specs=vmem,
        scratch_shapes=[
            pltpu.VMEM((3, PLANES, 2, 8, 128), f32),
            pltpu.VMEM((3, PLANES, 2, 8, 128), f32),
            pltpu.VMEM((PLANES, 2, 8, 128), f32),
            pltpu.VMEM((PLANES, 2, 8, 128), f32),
            pltpu.VMEM((PLANES, 2, 8, 128), f32),
            pltpu.VMEM((PLANES, 2, 8, 128), f32),
            pltpu.VMEM((PLANES, 2, 8, 128), f32),
            pltpu.VMEM((PLANES, 2, 8, 128), f32),
            pltpu.VMEM((3, 2, PLANES, 2, 8, 128), f32),
            pltpu.VMEM((3, 4, PLANES, 2, 8, 128), f32),
            pltpu.VMEM((3, 4, PLANES, 2, 8, 128), f32),
        ],
        compiler_params=params,
        name="iterate",
    )(lame_table, slots)
    back = swap(back, BACK)
    gaps = pl.pallas_call(
        gaps_kernel,
        out_shape=shape(count, 1, 128),
        in_specs=[vmem],
        out_specs=vmem,
        compiler_params=params,
        name="gaps",
    )(back)
    displacement, multiplier = pl.pallas_call(
        bricks_kernel,
        out_shape=(shape(*body_load.shape), shape(*body_load.shape)),
        in_specs=[vmem],
        out_specs=(vmem,) * 2,
        scratch_shapes=[pltpu.VMEM((2, 128, 128), f32)],
        compiler_params=params,
        cost_estimate=pl.CostEstimate(flops=0, bytes_accessed=1 << 22, transcendentals=0),
        name="bricks",
    )(back)
    gaps = lax.all_to_all(gaps, "gz", 0, 0, tiled=True)
    return (displacement, multiplier, jnp.max(gaps[:, 0, :ITERS], axis=0))


def solution(mesh):
    node, field = P("gx", "gy", "gz"), P(None, "gx", "gy", "gz")
    return jax.shard_map(
        shards,
        mesh=mesh,
        in_specs=(field, node, node, node, P()),
        out_specs=(field, field, P()),
        check_vma=False,
    )
```
